32 devices in a mesh: freq: 4 (over x, core), order: 8 (over z, y).
Axes of the slice: x: 2, y: 2, z: 4, core: 2. Of those that a mesh axis runs over, the one named last changes fastest.
Arguments:
- harmonics: bfloat16 [32, 16, 2, 4096], P(None, 'order'), may hold values from -6 to 6
- legendre: bfloat16 [16, 4096, 64], P('order'), may hold values from -0.09375 to 0.09375
- beam_window: float32 [4, 4096], replicated, may hold values from 0.2 to 1
- order_ids: int32 [16], replicated, may hold values from 0 to 4095, as said below
- noise_weight: float32 [4, 64, 8192], P('freq', 'order'), may hold values from 0.3 to 3
Outputs:
- applied: float32 [32, 16, 2, 4096], P('freq', 'order')
The draws below stay inside these ranges and needn't reach their ends.
Inputs may be any that keep to these rules, and one draw needn't show every extreme that they name: `order_ids`: all distinct; slots 2k and 2k + 1 hold the orders m and 4095 - m for some m < 2048; one pair holds the orders 0 and 4095.
All inputs are finite; a program needn't handle non-finite values.
Results may differ from the reference program's by a relative error of at most 0.0027.
Values may be sent and summed in bfloat16 or wider, within the bound.
A program may use at most 64 MiB of HBM per device.

```python
import math
import jax
import jax.numpy as jnp
from jax import lax

L = 4096
NLON = 8192
MAPS = 32
GROUPS = 4
ORDERS = 16
LATS = 64


def draw_order_ids(key, part):
    first_key, second_key = jax.random.split(jax.random.fold_in(key, 17))
    others = jax.random.permutation(first_key, L // 2 - 1)[:ORDERS // 2 - 1].astype(jnp.int32) + 1
    half = jnp.concatenate([jnp.zeros((1,), jnp.int32), others])
    half = jax.random.permutation(second_key, half)
    paired = jnp.stack([half, L - 1 - half], 1).reshape(-1)
    return paired.astype(jnp.int32)


def block_levels(own_key, shape, shards, smallest, top_value):
    level = 1.0
    for position, blocks in shards:
        draws = jax.random.uniform(jax.random.fold_in(jax.random.fold_in(own_key, 6), position), (blocks,), jnp.float32, smallest / len(shards), top_value / len(shards))
        level = level * jnp.repeat(jnp.exp(draws), shape[position] // blocks).reshape((-1,) + (1,) * (len(shape) - 1 - position))
    return level


def centred(own_key, dims, spread, bound, cuts=(), kind=jnp.bfloat16):
    drawn = jax.random.normal(own_key, dims, jnp.float32) * spread
    if len(cuts) > 0:
        drawn = block_levels(own_key, dims, cuts, -0.22, 0.18) * drawn
    return jnp.clip(drawn, min=-bound, max=bound).astype(kind)


def setup_inputs(seed: int = 0) -> dict:
    keys = jax.random.split(jax.random.key(seed), 6)
    return {
        "harmonics": centred(keys[0], (MAPS, ORDERS, 2, L), 1.0, 6.0, ((1, 8),)),
        "legendre": centred(keys[1], (ORDERS, L, LATS), L ** -0.5, 0.09375, ((0, 8),)),
        "beam_window": jnp.clip(jnp.exp(jax.random.uniform(keys[2], (GROUPS, L), jnp.float32, math.log(0.2), math.log(1.0))), 0.2, 1.0),
        "order_ids": draw_order_ids(jax.random.fold_in(keys[5], 71), 0),
        "noise_weight": jnp.clip(jnp.exp(math.log(3.0) - 2.3025851 * jax.random.uniform(keys[4], (GROUPS, LATS, NLON), jnp.float32) ** block_levels(keys[4], (GROUPS, LATS, NLON), ((0, 4), (1, 8)), -0.2, 0.2)), 0.3, 3.0),
    }


def make_table(order_ids, nlon):
    steps = jnp.arange(nlon, dtype=jnp.int32)
    turns = order_ids.astype(jnp.int32)[:, None] * steps[None, :] % nlon
    angle = turns.astype(jnp.float32) * (2.0 * math.pi / nlon)
    factor = jnp.where(order_ids == 0, 1.0, 2.0).astype(jnp.float32)[:, None]
    return jnp.stack([factor * jnp.cos(angle), -factor * jnp.sin(angle)], 1).astype(jnp.bfloat16)

def synthesize(smoothed, legendre):

    def one_order(pair):
        piece, values = pair
        out = jnp.dot(piece.reshape(-1, piece.shape[-1]), values, preferred_element_type=jnp.float32)
        return out.reshape(piece.shape[0], piece.shape[1], values.shape[1]).astype(jnp.bfloat16)
    stacked = lax.map(one_order, (jnp.moveaxis(smoothed, 1, 0), legendre))
    return jnp.moveaxis(stacked, 0, 1)

def analyze(band_terms, legendre):

    def one_order(pair):
        piece, values = pair
        out = jnp.dot(piece.reshape(-1, piece.shape[-1]), values.T, preferred_element_type=jnp.float32)
        return out.reshape(piece.shape[0], piece.shape[1], values.shape[0])
    stacked = lax.map(one_order, (jnp.moveaxis(band_terms, 1, 0), legendre))
    return jnp.moveaxis(stacked, 0, 1)

def reference(harmonics, legendre, beam_window, order_ids, noise_weight):
    live_mask = (jnp.arange(L, dtype=jnp.int32)[None, :] >= order_ids[:, None]).astype(jnp.float32)
    table_wide = make_table(order_ids, NLON).astype(jnp.float32)
    fwd_scale = 1.0 / math.sqrt(2.0 * ORDERS)
    back_scale = 1.0 / math.sqrt(1.0 * NLON)
    total = jnp.zeros((MAPS, ORDERS, 2, L), jnp.float32)
    for group in range(GROUPS):
        shaping = (beam_window[group][None, :] * live_mask)[None, :, None, :]
        smoothed = (harmonics.astype(jnp.float32) * shaping).astype(jnp.bfloat16)
        columns = synthesize(smoothed, legendre)
        field = jnp.einsum('bocr,ocj->brj', columns.astype(jnp.float32), table_wide, precision=lax.Precision.HIGHEST) * fwd_scale
        weighted = (field * noise_weight[group][None]).astype(jnp.bfloat16)
        band_terms = (jnp.einsum('brj,ocj->bocr', weighted.astype(jnp.float32), table_wide, precision=lax.Precision.HIGHEST) * back_scale).astype(jnp.bfloat16)
        total = total + analyze(band_terms, legendre) * shaping
    return total
```

```python
import functools
import math

import jax
import jax.numpy as jnp
from jax import lax
from jax.experimental import pallas as pl
from jax.experimental.pallas import tpu as pltpu
from jax.sharding import PartitionSpec as P

MESH = pl.DeviceIdType.MESH
NT = (((1,), (1,)), ((), ()))
LANES = 128
F32 = jnp.float32
BF16 = jnp.bfloat16


def sin_cos_turns(step, period):
    turns = step.astype(F32) * (4.0 / period)
    quarter = jnp.floor(turns + 0.5)
    x = (turns - quarter) * (0.5 * math.pi)
    y = x * x
    sin = x * (1.0 + y * (-1.0 / 6 + y * (1.0 / 120 + y * (-1.0 / 5040 + y * (1.0 / 362880)))))
    cos = 1.0 + y * (-0.5 + y * (1.0 / 24 + y * (-1.0 / 720 + y * (1.0 / 40320 - y * (1.0 / 3628800)))))
    quad = quarter.astype(jnp.int32) % 4
    odd = quad % 2 == 1
    c = jnp.where(odd, sin, cos)
    s = jnp.where(odd, cos, sin)
    c = jnp.where((quad == 1) | (quad == 2), -c, c)
    s = jnp.where(quad >= 2, -s, s)
    return c, s


def build_table(ids, wide, table, rows, nlon):
    shape = (rows, LANES)
    row = lax.broadcasted_iota(jnp.int32, shape, 0)
    lane = lax.broadcasted_iota(jnp.int32, shape, 1)
    order = jnp.zeros(shape, jnp.int32)
    for slot in range(rows // 2):
        order = jnp.where(row // 2 == slot, ids[slot], order)
    c, s = sin_cos_turns((order * lane + (row % 2) * (nlon // 4)) % nlon, nlon)
    factor = jnp.where(order == 0, 1.0, 2.0).astype(F32)
    c, s = c * factor, s * factor
    doublings = int(math.log2(nlon // LANES))
    reach = jnp.left_shift(LANES, jnp.minimum(lane, doublings))
    rc, rs = sin_cos_turns((order * reach) % nlon, nlon)
    cos_parts, sin_parts = [c], [s]
    for level in range(doublings):
        bc = jnp.broadcast_to(rc[:, level : level + 1], shape)
        bs = jnp.broadcast_to(rs[:, level : level + 1], shape)
        new_cos = [c * bc - s * bs for c, s in zip(cos_parts, sin_parts)]
        if level < doublings - 1:
            sin_parts = sin_parts + [s * bc + c * bs for c, s in zip(cos_parts, sin_parts)]
        cos_parts = cos_parts + new_cos
    for part, c in enumerate(cos_parts):
        rounded = c.astype(BF16)
        table[:, part * LANES : (part + 1) * LANES] = rounded
        wide[:, part * LANES : (part + 1) * LANES] = rounded.astype(F32)


def gather_kernel(
    nf, no, ids, beam, harm_hbm, leg_hbm, noise_hbm, z_ref,
    harm, leg, noise, wide, table, gram, spread, xs, xr, vs, vr, flipped,
    load_sem, send1, recv1, send2, recv2,
):
    maps, od, _, degrees = harm.shape
    lats, nlon = noise.shape[1], noise.shape[2]
    all_lats = leg.shape[1]
    rows = no * od * 2
    half = maps * 2
    total = nf * no
    myf, me = lax.axis_index("freq"), lax.axis_index("order")
    lin = myf * no + me

    loads = [
        pltpu.make_async_copy(harm_hbm, harm, load_sem.at[0]),
        pltpu.make_async_copy(leg_hbm, leg, load_sem.at[1]),
        pltpu.make_async_copy(noise_hbm, noise, load_sem.at[2]),
    ]
    for load in loads:
        load.start()

    barrier = pltpu.get_barrier_semaphore()

    def greet(k, carry):
        to = (lin + k) % total
        pl.semaphore_signal(barrier, inc=1, device_id=(to // no, to % no), device_id_type=MESH)
        return carry

    lax.fori_loop(1, total, greet, 0)

    build_table(ids, wide, table, rows, nlon)

    own_beam = beam[pl.ds(myf, 1), :]
    loads[0].wait()
    loads[1].wait()
    step = 512
    parts = []
    for o in range(od):
        degree = lax.broadcasted_iota(jnp.int32, (1, degrees), 1)
        shaping = jnp.where(degree >= ids[me * od + o], own_beam, 0.0)
        acc = jnp.zeros((all_lats, half), F32)
        for at in range(0, degrees, step):
            cut = slice(at, at + step)
            piece = harm[:, o, :, cut].astype(F32) * shaping[:, cut].reshape(1, 1, step)
            piece = piece.reshape(half, step).astype(BF16)
            acc = acc + lax.dot_general(leg[o, :, cut], piece, NT, preferred_element_type=F32)
        parts.append(acc)
    columns = jnp.concatenate(parts, axis=1).astype(BF16).astype(F32)
    xs[...] = columns.reshape(no, lats, od * half)
    xr[me] = xs[me]

    pl.semaphore_wait(barrier, total - 1)

    def copy1(k):
        to = (me + k) % no
        return pltpu.make_async_remote_copy(
            xs.at[to], xr.at[me], send1.at[to], recv1.at[me],
            device_id=(myf, to), device_id_type=MESH,
        )

    def arrive1(k):
        frm = (me + k) % no
        return pltpu.make_async_remote_copy(
            xs.at[frm], xr.at[frm], send1.at[frm], recv1.at[frm],
            device_id=(myf, frm), device_id_type=MESH,
        )

    lax.fori_loop(1, no, lambda k, c: (copy1(k).start(), c)[1], 0)

    loads[2].wait()
    wide_step = 1024

    def gram_step(i, acc):
        cut = pl.ds(pl.multiple_of(i * wide_step, wide_step), wide_step)
        left = wide[:, cut][:, None, :] * noise[0, :, cut][None, :, :]
        left = left.reshape(rows * lats, wide_step).astype(BF16)
        return acc + lax.dot_general(left, table[:, cut], NT, preferred_element_type=F32)

    acc = lax.fori_loop(
        0, nlon // wide_step, gram_step, jnp.zeros((rows * lats, rows), F32)
    )
    gram[...] = acc * (1.0 / math.sqrt(2.0 * no * od) / math.sqrt(1.0 * nlon))

    span = no * LANES
    p = lax.broadcasted_iota(jnp.int32, (rows, span), 0)
    q = lax.broadcasted_iota(jnp.int32, (rows, span), 1)
    lane_q = q % LANES
    fan = (p == (q // LANES) * (2 * od) + (lane_q // half) * 2 + lane_q % 2).astype(F32).astype(BF16)

    def expand(value):
        high = value.astype(BF16)
        low = (value - high.astype(F32)).astype(BF16)
        return jnp.dot(high, fan, preferred_element_type=F32) + jnp.dot(
            low, fan, preferred_element_type=F32
        )

    ahead = spread.shape[0] == rows * lats
    if ahead:
        spread[...] = expand(gram[...])

    def settle1(k, c):
        arrive1(k).wait_recv()
        return c

    lax.fori_loop(1, no, settle1, 0)

    lane = lax.broadcasted_iota(jnp.int32, (lats, LANES), 1)
    even = lane % 2 == 0
    first = lane < half

    def mix(d, get):
        sums = []
        for s in range(2 * od):
            t = get(s, 0) * xr[0]
            for o in range(1, no):
                t = t + get(s, o) * xr[o]
            t = t + pltpu.roll(t, half, 1)
            t = t + jnp.where(even, pltpu.roll(t, LANES - 1, 1), pltpu.roll(t, 1, 1))
            sums.append(t)
        out = jnp.where(first, jnp.where(even, sums[0], sums[1]), jnp.where(even, sums[2], sums[3]))
        vs[d] = out.astype(BF16).astype(F32)

    group = 2 * od * lats
    if ahead:
        for d in range(no):
            mix(d, lambda s, o: spread[d * group + s * lats : d * group + (s + 1) * lats, o * LANES : (o + 1) * LANES])
    else:
        def late(d, c):
            spread[...] = expand(gram[pl.ds(pl.multiple_of(d * group, group), group), :])
            mix(d, lambda s, o: spread[s * lats : (s + 1) * lats, o * LANES : (o + 1) * LANES])
            return c
        lax.fori_loop(0, no, late, 0)

    vr[myf, me] = vs[me]

    def copy2(k):
        to = (lin + k) % total
        return pltpu.make_async_remote_copy(
            vs.at[to % no], vr.at[myf, me], send2.at[to], recv2.at[lin],
            device_id=(to // no, to % no), device_id_type=MESH,
        )

    def arrive2(k):
        frm = (lin + k) % total
        return pltpu.make_async_remote_copy(
            vs.at[frm % no], vr.at[frm // no, frm % no], send2.at[frm], recv2.at[frm],
            device_id=(frm // no, frm % no), device_id_type=MESH,
        )

    lax.fori_loop(1, total, lambda k, c: (copy2(k).start(), c)[1], 0)

    def settle2(k, c):
        arrive2(k).wait_recv()
        return c

    lax.fori_loop(1, total, settle2, 0)

    keep = half // nf
    for f in range(nf):
        flipped[f] = vr[f].reshape(all_lats, od * half).T
        for o in range(od):
            at = pl.multiple_of(o * half + myf * keep, keep)
            z_ref[o, f] = flipped[f, pl.ds(at, keep), :].astype(BF16)

    def drain(k, c):
        copy2(k).wait_send()
        return c

    lax.fori_loop(1, no, lambda k, c: (copy1(k).wait_send(), c)[1], 0)
    lax.fori_loop(1, total, drain, 0)


def project_kernel(ids, z_ref, beam, leg, out):
    od, nf, keep, all_lats = z_ref.shape
    width = leg.shape[2]
    me = lax.axis_index("order")
    degree = lax.broadcasted_iota(jnp.int32, (1, width), 1) + pl.program_id(0) * width
    for o in range(od):
        wide = jnp.dot(
            z_ref[o].reshape(nf * keep, all_lats), leg[o], preferred_element_type=F32
        )
        total = wide[0:keep] * beam[0:1, :]
        for f in range(1, nf):
            total = total + wide[f * keep : (f + 1) * keep] * beam[f : f + 1, :]
        total = jnp.where(degree >= ids[me * od + o], total, 0.0)
        out[:, o] = total.reshape(keep // 2, 2, width)


def on_device(nf, no, harmonics, legendre, beam_window, order_ids, noise_weight):
    maps, od, _, degrees = harmonics.shape
    _, lats, nlon = noise_weight.shape
    all_lats = legendre.shape[2]
    rows, half, total = no * od * 2, maps * 2, nf * no
    keep = half // nf
    leg = jnp.swapaxes(legendre, 1, 2)
    smem = pl.BlockSpec(memory_space=pltpu.SMEM)
    vmem = pl.BlockSpec(memory_space=pltpu.VMEM)
    hbm = pl.BlockSpec(memory_space=pl.ANY)
    span = no * LANES
    ahead = rows * lats * span * 4 <= 8 * 2**20
    dma = pltpu.SemaphoreType.DMA
    z = pl.pallas_call(
        functools.partial(gather_kernel, nf, no),
        out_shape=jax.ShapeDtypeStruct((od, nf, keep, all_lats), BF16),
        in_specs=[smem, vmem, hbm, hbm, hbm],
        out_specs=vmem,
        scratch_shapes=[
            pltpu.VMEM(harmonics.shape, BF16),
            pltpu.VMEM(leg.shape, BF16),
            pltpu.VMEM(noise_weight.shape, F32),
            pltpu.VMEM((rows, nlon), F32),
            pltpu.VMEM((rows, nlon), BF16),
            pltpu.VMEM((rows * lats, rows), F32),
            pltpu.VMEM((rows * lats if ahead else 2 * od * lats, span), F32),
            pltpu.VMEM((no, lats, od * half), F32),
            pltpu.VMEM((no, lats, od * half), F32),
            pltpu.VMEM((no, lats, od * half), F32),
            pltpu.VMEM((nf, no, lats, od * half), F32),
            pltpu.VMEM((nf, od * half, all_lats), F32),
            dma((3,)),
            dma((no,)),
            dma((no,)),
            dma((total,)),
            dma((total,)),
        ],
        compiler_params=pltpu.CompilerParams(
            collective_id=0, has_side_effects=True, vmem_limit_bytes=52 * 2**20
        ),
        name="exchange",
    )(order_ids, beam_window, harmonics, leg, noise_weight)
    width = 1024
    return pl.pallas_call(
        project_kernel,
        grid=(degrees // width,),
        out_shape=jax.ShapeDtypeStruct((maps // nf, od, 2, degrees), F32),
        in_specs=[
            smem,
            pl.BlockSpec(z.shape, lambda i: (0, 0, 0, 0)),
            pl.BlockSpec((nf, width), lambda i: (0, i)),
            pl.BlockSpec((od, all_lats, width), lambda i: (0, 0, i)),
        ],
        out_specs=pl.BlockSpec((maps // nf, od, 2, width), lambda i: (0, 0, 0, i)),
        compiler_params=pltpu.CompilerParams(vmem_limit_bytes=32 * 2**20),
        name="project",
    )(order_ids, z, beam_window, leg)


def solution(mesh):
    sizes = dict(mesh.shape)
    return jax.shard_map(
        functools.partial(on_device, sizes["freq"], sizes["order"]),
        mesh=mesh,
        in_specs=(
            P(None, "order", None, None),
            P("order", None, None),
            P(),
            P(),
            P("freq", "order", None),
        ),
        out_specs=P("freq", "order", None, None),
        check_vma=False,
    )
```

```python
import functools
import math

import jax
import jax.numpy as jnp
from jax import lax
from jax.experimental import pallas as pl
from jax.experimental.pallas import tpu as pltpu
from jax.sharding import PartitionSpec as P

MESH = pl.DeviceIdType.MESH
NT = (((1,), (1,)), ((), ()))
LANES = 128
F32 = jnp.float32
BF16 = jnp.bfloat16


def sin_cos_turns(step, period):
    turns = step.astype(F32) * (4.0 / period)
    quarter = jnp.floor(turns + 0.5)
    x = (turns - quarter) * (0.5 * math.pi)
    y = x * x
    sin = x * (1.0 + y * (-1.0 / 6 + y * (1.0 / 120 + y * (-1.0 / 5040 + y * (1.0 / 362880)))))
    cos = 1.0 + y * (-0.5 + y * (1.0 / 24 + y * (-1.0 / 720 + y * (1.0 / 40320 - y * (1.0 / 3628800)))))
    quad = quarter.astype(jnp.int32) % 4
    odd = quad % 2 == 1
    c = jnp.where(odd, sin, cos)
    s = jnp.where(odd, cos, sin)
    c = jnp.where((quad == 1) | (quad == 2), -c, c)
    s = jnp.where(quad >= 2, -s, s)
    return c, s


def build_table(ids, wide, table, rows, nlon):
    shape = (rows, LANES)
    row = lax.broadcasted_iota(jnp.int32, shape, 0)
    lane = lax.broadcasted_iota(jnp.int32, shape, 1)
    order = jnp.zeros(shape, jnp.int32)
    for slot in range(rows // 2):
        order = jnp.where(row // 2 == slot, ids[slot], order)
    c, s = sin_cos_turns((order * lane + (row % 2) * (nlon // 4)) % nlon, nlon)
    factor = jnp.where(order == 0, 1.0, 2.0).astype(F32)
    c, s = c * factor, s * factor
    doublings = int(math.log2(nlon // LANES))
    reach = jnp.left_shift(LANES, jnp.minimum(lane, doublings))
    rc, rs = sin_cos_turns((order * reach) % nlon, nlon)
    cos_parts, sin_parts = [c], [s]
    for level in range(doublings):
        bc = jnp.broadcast_to(rc[:, level : level + 1], shape)
        bs = jnp.broadcast_to(rs[:, level : level + 1], shape)
        new_cos = [c * bc - s * bs for c, s in zip(cos_parts, sin_parts)]
        if level < doublings - 1:
            sin_parts = sin_parts + [s * bc + c * bs for c, s in zip(cos_parts, sin_parts)]
        cos_parts = cos_parts + new_cos
    for part, c in enumerate(cos_parts):
        rounded = c.astype(BF16)
        table[:, part * LANES : (part + 1) * LANES] = rounded
        wide[:, part * LANES : (part + 1) * LANES] = rounded.astype(F32)


def wrap(value, n):
    return jnp.where(value >= n, value - n, value)


def gather_kernel(
    nf, no, ids_hbm, beam_hbm, harm_hbm, leg_hbm, noise_hbm, out,
    ids, beam, harm, leg, noise, flat, wide, table, gram, spread, xs, xr, vs, vr, flipped,
    shaping_ref, stage, load_sem, send1, recv1, send2, recv2, out_sem,
):
    maps, od, tiles2, _ = harm.shape
    tiles = tiles2 // 2
    lats, nlon = noise.shape[1], noise.shape[2]
    all_lats = leg.shape[1]
    rows = no * od * 2
    half = maps * 2
    total = nf * no
    myf, me = lax.axis_index("freq"), lax.axis_index("order")
    lin = myf * no + me

    def peers_order(act):
        if no <= 16:
            for k in range(1, no):
                act(wrap(me + k, no))
        else:
            lax.fori_loop(1, no, lambda k, c: (act(wrap(me + k, no)), c)[1], 0)

    def peers_all(act):
        for g in range(nf):
            f = wrap(myf + g, nf)
            low = 1 if g == 0 else 0
            if total <= 64:
                for k in range(low, no):
                    act(f, wrap(me + k, no))
            else:
                lax.fori_loop(low, no, lambda k, c: (act(f, wrap(me + k, no)), c)[1], 0)

    loads = [
        pltpu.make_async_copy(ids_hbm, ids, load_sem.at[0]),
        pltpu.make_async_copy(harm_hbm, harm, load_sem.at[1]),
        pltpu.make_async_copy(beam_hbm, beam, load_sem.at[2]),
        pltpu.make_async_copy(leg_hbm, leg, load_sem.at[3]),
        pltpu.make_async_copy(noise_hbm, noise, load_sem.at[4]),
    ]
    for load in loads:
        load.start()

    barrier = pltpu.get_barrier_semaphore()

    def greet(f, o):
        pl.semaphore_signal(barrier, inc=1, device_id=(f, o), device_id_type=MESH)

    peers_all(greet)

    loads[0].wait()
    build_table(ids, wide, table, rows, nlon)

    loads[2].wait()
    degrees = beam.shape[1]
    degree = lax.broadcasted_iota(jnp.int32, (1, degrees), 1)
    for o in range(od):
        shaping_ref[o] = jnp.where(degree >= ids[me * od + o], beam[...], 0.0)
    loads[1].wait()
    loads[3].wait()
    step = 4
    parts = []
    for o in range(od):
        flat[o] = harm[:, o].astype(F32).reshape(maps * tiles2, LANES)
        shaping = shaping_ref[o, pl.ds(myf, 1), :]
        acc = jnp.zeros((all_lats, half), F32)
        for at in range(0, tiles, step):
            piece = jnp.concatenate(
                [
                    jnp.concatenate(
                        [
                            flat[o, pl.ds(t * 2 + c, maps, stride=tiles2), :]
                            * shaping[:, t * LANES : (t + 1) * LANES]
                            for t in range(at, at + step)
                        ],
                        axis=1,
                    )
                    for c in range(2)
                ],
                axis=0,
            ).astype(BF16)
            cut = slice(at * LANES, (at + step) * LANES)
            acc = acc + lax.dot_general(leg[o, :, cut], piece, NT, preferred_element_type=F32)
        parts.append(acc)
    columns = jnp.concatenate(parts, axis=1).astype(BF16).astype(F32)
    xs[...] = columns.reshape(no, lats, od * half)
    xr[me] = xs[me]

    pl.semaphore_wait(barrier, total - 1)

    def copy1(to):
        return pltpu.make_async_remote_copy(
            xs.at[to], xr.at[me], send1.at[to], recv1.at[me],
            device_id=(myf, to), device_id_type=MESH,
        )

    def arrive1(frm):
        pltpu.make_async_remote_copy(
            xs.at[frm], xr.at[frm], send1.at[frm], recv1.at[frm],
            device_id=(myf, frm), device_id_type=MESH,
        ).wait_recv()

    peers_order(lambda to: copy1(to).start())

    loads[4].wait()
    wide_step = 1024

    def gram_step(i, acc):
        cut = pl.ds(pl.multiple_of(i * wide_step, wide_step), wide_step)
        left = wide[:, cut][:, None, :] * noise[0, :, cut][None, :, :]
        left = left.reshape(rows * lats, wide_step).astype(BF16)
        return acc + lax.dot_general(left, table[:, cut], NT, preferred_element_type=F32)

    acc = lax.fori_loop(
        0, nlon // wide_step, gram_step, jnp.zeros((rows * lats, rows), F32)
    )
    gram[...] = acc * (1.0 / math.sqrt(2.0 * no * od) / math.sqrt(1.0 * nlon))

    span = no * LANES
    p = lax.broadcasted_iota(jnp.int32, (rows, span), 0)
    q = lax.broadcasted_iota(jnp.int32, (rows, span), 1)
    fan = (p == q // maps).astype(F32).astype(BF16)

    def expand(value):
        high = value.astype(BF16)
        low = (value - high.astype(F32)).astype(BF16)
        return jnp.dot(high, fan, preferred_element_type=F32) + jnp.dot(
            low, fan, preferred_element_type=F32
        )

    ahead = spread.shape[0] == rows * lats
    if ahead:
        spread[...] = expand(gram[...])

    peers_order(arrive1)

    part = lax.broadcasted_iota(jnp.int32, (lats, LANES), 1) // maps

    def mix(d, get):
        out = None
        for s in range(2 * od):
            t = get(s, 0) * xr[0]
            for o in range(1, no):
                t = t + get(s, o) * xr[o]
            t = t + pltpu.roll(t, half, 1)
            t = t + pltpu.roll(t, maps, 1)
            out = t if out is None else jnp.where(part == s, t, out)
        vs[d] = out.astype(BF16).astype(F32)

    group = 2 * od * lats
    if ahead:
        for d in range(no):
            mix(d, lambda s, o: spread[d * group + s * lats : d * group + (s + 1) * lats, o * LANES : (o + 1) * LANES])
    else:
        def late(d, c):
            spread[...] = expand(gram[pl.ds(pl.multiple_of(d * group, group), group), :])
            mix(d, lambda s, o: spread[s * lats : (s + 1) * lats, o * LANES : (o + 1) * LANES])
            return c
        lax.fori_loop(0, no, late, 0)

    vr[myf, me] = vs[me]

    def copy2(f, o):
        return pltpu.make_async_remote_copy(
            vs.at[o], vr.at[myf, me], send2.at[f * no + o], recv2.at[lin],
            device_id=(f, o), device_id_type=MESH,
        )

    def arrive2(f, o):
        frm = f * no + o
        pltpu.make_async_remote_copy(
            vs.at[o], vr.at[f, o], send2.at[frm], recv2.at[frm],
            device_id=(f, o), device_id_type=MESH,
        ).wait_recv()

    peers_all(lambda f, o: copy2(f, o).start())
    peers_all(arrive2)

    keep = maps // nf
    for f in range(nf):
        flipped[f] = vr[f].reshape(all_lats, od * half).T

    width = 1024
    copies = []
    for o in range(od):
        pieces = []
        for f in range(nf):
            for c in range(2):
                at = pl.multiple_of(o * half + c * maps + myf * keep, keep)
                pieces.append(flipped[f, pl.ds(at, keep), :])
        z = jnp.concatenate(pieces, axis=0).astype(BF16)
        for at in range(0, degrees, width):
            cut = slice(at, at + width)
            terms = jnp.dot(z, leg[o, :, cut], preferred_element_type=F32)
            sums = terms[0 : 2 * keep] * shaping_ref[o, 0:1, cut]
            for f in range(1, nf):
                sums = sums + terms[f * 2 * keep : (f + 1) * 2 * keep] * shaping_ref[o, f : f + 1, cut]
            for t in range(width // LANES):
                for c in range(2):
                    row = (at // LANES + t) * 2 + c
                    stage[o, pl.ds(row, keep, stride=tiles2), :] = sums[
                        c * keep : (c + 1) * keep, t * LANES : (t + 1) * LANES
                    ]
        for b in range(keep):
            copy = pltpu.make_async_copy(
                stage.at[o, pl.ds(b * tiles2, tiles2)], out.at[b, o], out_sem.at[o, b]
            )
            copy.start()
            copies.append(copy)

    peers_order(lambda to: copy1(to).wait_send())
    peers_all(lambda f, o: copy2(f, o).wait_send())
    for copy in copies:
        copy.wait()


def on_device(nf, no, harmonics, legendre, beam_window, order_ids, noise_weight):
    maps, od, _, degrees = harmonics.shape
    _, lats, nlon = noise_weight.shape
    all_lats = legendre.shape[2]
    rows, half, total = no * od * 2, maps * 2, nf * no
    keep = maps // nf
    tiles = degrees // LANES
    leg = jnp.swapaxes(legendre, 1, 2)
    harm = harmonics.reshape(maps, od, 2, tiles, LANES)
    harm = jnp.swapaxes(harm, 2, 3).reshape(maps, od, tiles * 2, LANES)
    hbm = pl.BlockSpec(memory_space=pltpu.HBM)
    span = no * LANES
    ahead = rows * lats * span * 4 <= 8 * 2**20
    dma = pltpu.SemaphoreType.DMA
    out = pl.pallas_call(
        functools.partial(gather_kernel, nf, no),
        out_shape=jax.ShapeDtypeStruct((keep, od, tiles * 2, LANES), F32),
        in_specs=[hbm, hbm, hbm, hbm, hbm],
        out_specs=hbm,
        scratch_shapes=[
            pltpu.SMEM(order_ids.shape, jnp.int32),
            pltpu.VMEM(beam_window.shape, F32),
            pltpu.VMEM(harm.shape, BF16),
            pltpu.VMEM(leg.shape, BF16),
            pltpu.VMEM(noise_weight.shape, F32),
            pltpu.VMEM((od, maps * tiles * 2, LANES), F32),
            pltpu.VMEM((rows, nlon), F32),
            pltpu.VMEM((rows, nlon), BF16),
            pltpu.VMEM((rows * lats, rows), F32),
            pltpu.VMEM((rows * lats if ahead else 2 * od * lats, span), F32),
            pltpu.VMEM((no, lats, od * half), F32),
            pltpu.VMEM((no, lats, od * half), F32),
            pltpu.VMEM((no, lats, od * half), F32),
            pltpu.VMEM((nf, no, lats, od * half), F32),
            pltpu.VMEM((nf, od * half, all_lats), F32),
            pltpu.VMEM((od, nf, degrees), F32),
            pltpu.VMEM((od, keep * tiles * 2, LANES), F32),
            dma((5,)),
            dma((no,)),
            dma((no,)),
            dma((total,)),
            dma((total,)),
            dma((od, keep)),
        ],
        compiler_params=pltpu.CompilerParams(
            collective_id=0, has_side_effects=True, vmem_limit_bytes=60 * 2**20
        ),
        name="operator",
    )(order_ids, beam_window, harm, leg, noise_weight)
    out = jnp.swapaxes(out.reshape(keep, od, tiles, 2, LANES), 2, 3)
    return out.reshape(keep, od, 2, degrees)


def solution(mesh):
    sizes = dict(mesh.shape)
    return jax.shard_map(
        functools.partial(on_device, sizes["freq"], sizes["order"]),
        mesh=mesh,
        in_specs=(
            P(None, "order", None, None),
            P("order", None, None),
            P(),
            P(),
            P("freq", "order", None),
        ),
        out_specs=P("freq", "order", None, None),
        check_vma=False,
    )
```

```python
import functools
import math

import jax
import jax.numpy as jnp
from jax import lax
from jax.experimental import pallas as pl
from jax.experimental.pallas import tpu as pltpu
from jax.sharding import PartitionSpec as P

MESH = pl.DeviceIdType.MESH
NT = (((1,), (1,)), ((), ()))
LANES = 128
F32 = jnp.float32
BF16 = jnp.bfloat16


def sin_cos_turns(step, period):
    turns = step.astype(F32) * (4.0 / period)
    quarter = jnp.floor(turns + 0.5)
    x = (turns - quarter) * (0.5 * math.pi)
    y = x * x
    sin = x * (1.0 + y * (-1.0 / 6 + y * (1.0 / 120 + y * (-1.0 / 5040 + y * (1.0 / 362880)))))
    cos = 1.0 + y * (-0.5 + y * (1.0 / 24 + y * (-1.0 / 720 + y * (1.0 / 40320 - y * (1.0 / 3628800)))))
    quad = quarter.astype(jnp.int32) & 3
    odd = (quad & 1) == 1
    c = jnp.where(odd, sin, cos)
    s = jnp.where(odd, cos, sin)
    c = jnp.where((quad == 1) | (quad == 2), -c, c)
    s = jnp.where(quad >= 2, -s, s)
    return c, s


def build_table(ids, wide, table, rows, nlon):
    shape = (rows, LANES)
    row = lax.broadcasted_iota(jnp.int32, shape, 0)
    lane = lax.broadcasted_iota(jnp.int32, shape, 1)
    order = jnp.zeros(shape, jnp.int32)
    for slot in range(rows // 2):
        order = jnp.where(row >= 2 * slot, ids[slot], order)
    c, s = sin_cos_turns(lax.rem(order * lane + (row & 1) * (nlon // 4), nlon), nlon)
    factor = jnp.where(order == 0, 1.0, 2.0).astype(F32)
    c, s = c * factor, s * factor
    doublings = int(math.log2(nlon // LANES))
    reach = jnp.left_shift(LANES, jnp.minimum(lane, doublings))
    rc, rs = sin_cos_turns(lax.rem(order * reach, nlon), nlon)
    cos_parts, sin_parts = [c], [s]
    for level in range(doublings):
        bc = jnp.broadcast_to(rc[:, level : level + 1], shape)
        bs = jnp.broadcast_to(rs[:, level : level + 1], shape)
        new_cos = [c * bc - s * bs for c, s in zip(cos_parts, sin_parts)]
        if level < doublings - 1:
            sin_parts = sin_parts + [s * bc + c * bs for c, s in zip(cos_parts, sin_parts)]
        cos_parts = cos_parts + new_cos
    for part, c in enumerate(cos_parts):
        rounded = c.astype(BF16)
        table[:, part * LANES : (part + 1) * LANES] = rounded
        wide[:, part * LANES : (part + 1) * LANES] = rounded.astype(F32)


def wrap(value, n):
    return jnp.where(value >= n, value - n, value)


def gather_kernel(
    nf, no, ids_hbm, beam_hbm, harm_hbm, leg_hbm, noise_hbm, out,
    ids, beam, harm, leg, noise, flat, wide, table, gram, fan, spread, xs, xr, vs, vr, flipped,
    shaping_ref, stage, load_sem, send1, recv1, send2, recv2, out_sem,
):
    maps, od, tiles2, _ = harm.shape
    tiles = tiles2 // 2
    lats, nlon = noise.shape[1], noise.shape[2]
    all_lats = leg.shape[1]
    rows = no * od * 2
    half = maps * 2
    total = nf * no
    myf, me = lax.axis_index("freq"), lax.axis_index("order")
    lin = myf * no + me

    def peers_order(act):
        if no <= 16:
            for k in range(1, no):
                act(wrap(me + k, no))
        else:
            lax.fori_loop(1, no, lambda k, c: (act(wrap(me + k, no)), c)[1], 0)

    def peers_all(act):
        for g in range(nf):
            f = wrap(myf + g, nf)
            low = 1 if g == 0 else 0
            if total <= 64:
                for k in range(low, no):
                    act(f, wrap(me + k, no))
            else:
                lax.fori_loop(low, no, lambda k, c: (act(f, wrap(me + k, no)), c)[1], 0)

    loads = [
        pltpu.make_async_copy(ids_hbm, ids, load_sem.at[0]),
        pltpu.make_async_copy(harm_hbm, harm, load_sem.at[1]),
        pltpu.make_async_copy(beam_hbm, beam, load_sem.at[2]),
        pltpu.make_async_copy(leg_hbm, leg, load_sem.at[3]),
        pltpu.make_async_copy(noise_hbm, noise, load_sem.at[4]),
    ]
    for load in loads:
        load.start()

    barrier = pltpu.get_barrier_semaphore()

    def greet(f, o):
        pl.semaphore_signal(barrier, inc=1, device_id=(f, o), device_id_type=MESH)

    peers_all(greet)

    loads[0].wait()
    build_table(ids, wide, table, rows, nlon)

    span = no * LANES
    p = lax.broadcasted_iota(jnp.int32, (rows, span), 0) * maps
    q = lax.broadcasted_iota(jnp.int32, (rows, span), 1)
    fan_half = ((q >= p) & (q < p + maps)).astype(F32).astype(BF16)
    fan[...] = jnp.concatenate([fan_half, fan_half], axis=0)

    loads[2].wait()
    degrees = beam.shape[1]
    degree = lax.broadcasted_iota(jnp.int32, (1, degrees), 1)
    for o in range(od):
        shaping_ref[o] = jnp.where(degree >= ids[me * od + o], beam[...], 0.0)
    loads[1].wait()
    loads[3].wait()
    step = 4
    parts = []
    for o in range(od):
        flat[o] = harm[:, o].astype(F32).reshape(maps * tiles2, LANES)
        shaping = shaping_ref[o, pl.ds(myf, 1), :]
        acc = jnp.zeros((all_lats, half), F32)
        for at in range(0, tiles, step):
            piece = jnp.concatenate(
                [
                    jnp.concatenate(
                        [
                            flat[o, pl.ds(t * 2 + c, maps, stride=tiles2), :]
                            * shaping[:, t * LANES : (t + 1) * LANES]
                            for t in range(at, at + step)
                        ],
                        axis=1,
                    )
                    for c in range(2)
                ],
                axis=0,
            ).astype(BF16)
            cut = slice(at * LANES, (at + step) * LANES)
            acc = acc + lax.dot_general(leg[o, :, cut], piece, NT, preferred_element_type=F32)
        parts.append(acc)
    columns = jnp.concatenate(parts, axis=1).astype(BF16).astype(F32)
    xs[...] = columns.reshape(no, lats, od * half)
    xr[me] = xs[me]

    pl.semaphore_wait(barrier, total - 1)

    def copy1(to):
        return pltpu.make_async_remote_copy(
            xs.at[to], xr.at[me], send1.at[to], recv1.at[me],
            device_id=(myf, to), device_id_type=MESH,
        )

    def arrive1(frm):
        pltpu.make_async_remote_copy(
            xs.at[frm], xr.at[frm], send1.at[frm], recv1.at[frm],
            device_id=(myf, frm), device_id_type=MESH,
        ).wait_recv()

    peers_order(lambda to: copy1(to).start())

    loads[4].wait()
    wide_step = 1024

    def gram_step(i, acc):
        cut = pl.ds(pl.multiple_of(i * wide_step, wide_step), wide_step)
        weight = noise[0, :, cut]
        left = [(wide[row : row + 1, cut] * weight) for row in range(rows)]
        left = jnp.concatenate(left, axis=0).astype(BF16)
        return acc + lax.dot_general(left, table[:, cut], NT, preferred_element_type=F32)

    acc = lax.fori_loop(
        0, nlon // wide_step, gram_step, jnp.zeros((rows * lats, rows), F32)
    )
    gram[...] = acc * (1.0 / math.sqrt(2.0 * no * od) / math.sqrt(1.0 * nlon))

    def expand(value):
        high = value.astype(BF16)
        low = (value - high.astype(F32)).astype(BF16)
        both = jnp.concatenate([high, low], axis=1)
        return jnp.dot(both, fan[...], preferred_element_type=F32)

    ahead = spread.shape[0] == rows * lats
    if ahead:
        spread[...] = expand(gram[...])

    peers_order(arrive1)

    keep = maps // nf
    folds = lats // nf
    lane = lax.broadcasted_iota(jnp.int32, (lats, LANES), 1)
    sub = lax.broadcasted_iota(jnp.int32, (lats, LANES), 0)
    part = lane // maps
    slot = lax.rem(lane, maps) // keep
    own_slot = slot == lax.rem(sub, nf)

    def pack(d, value):
        turned = [value]
        for k in range(1, nf):
            turned.append(
                jnp.where(
                    slot >= k,
                    pltpu.roll(value, k * keep, 1),
                    pltpu.roll(value, LANES + k * keep - maps, 1),
                )
            )
        for f in range(nf):
            own = turned[-f % nf]
            for at in range(1, nf):
                own = jnp.where(slot == at, turned[(at - f) % nf], own)
            own = jnp.where(own_slot, own, 0.0)
            shift = 1
            while shift < nf:
                own = own + pltpu.roll(own, lats - shift, 0)
                shift *= 2
            for row in range(folds):
                vs[f, d, row : row + 1, :] = own[row * nf : row * nf + 1]

    def unpack(f, o):
        value = jnp.broadcast_to(vr[f, o, 0:1, :], (lats, LANES))
        for row in range(1, folds):
            value = jnp.where(sub >= row * nf, jnp.broadcast_to(vr[f, o, row : row + 1, :], (lats, LANES)), value)
        value = jnp.where(own_slot, value, 0.0)
        shift = 1
        while shift < nf:
            value = value + pltpu.roll(value, LANES - shift * keep, 1)
            shift *= 2
        return value

    def mix(d, get):
        out = None
        for s in range(2 * od):
            t = get(s, 0) * xr[0]
            for o in range(1, no):
                t = t + get(s, o) * xr[o]
            t = t + pltpu.roll(t, half, 1)
            t = t + pltpu.roll(t, maps, 1)
            out = t if out is None else jnp.where(part == s, t, out)
        pack(d, out.astype(BF16).astype(F32))

    group = 2 * od * lats
    if ahead:
        for d in range(no):
            mix(d, lambda s, o: spread[d * group + s * lats : d * group + (s + 1) * lats, o * LANES : (o + 1) * LANES])
    else:
        def late(d, c):
            spread[...] = expand(gram[pl.ds(pl.multiple_of(d * group, group), group), :])
            mix(d, lambda s, o: spread[s * lats : (s + 1) * lats, o * LANES : (o + 1) * LANES])
            return c
        lax.fori_loop(0, no, late, 0)

    vr[myf, me] = vs[myf, me]

    def copy2(f, o):
        return pltpu.make_async_remote_copy(
            vs.at[f, o], vr.at[myf, me], send2.at[f * no + o], recv2.at[lin],
            device_id=(f, o), device_id_type=MESH,
        )

    def arrive2(f, o):
        frm = f * no + o
        pltpu.make_async_remote_copy(
            vs.at[f, o], vr.at[f, o], send2.at[frm], recv2.at[frm],
            device_id=(f, o), device_id_type=MESH,
        ).wait_recv()

    peers_all(lambda f, o: copy2(f, o).start())
    peers_all(arrive2)

    for f in range(nf):
        flipped[f] = jnp.concatenate([unpack(f, o) for o in range(no)], axis=0).T

    width = 1024
    copies = []
    for o in range(od):
        pieces = []
        for f in range(nf):
            for c in range(2):
                at = o * half + c * maps
                pieces.append(flipped[f, at : at + keep, :])
        z = jnp.concatenate(pieces, axis=0).astype(BF16)
        for at in range(0, degrees, width):
            cut = slice(at, at + width)
            terms = jnp.dot(z, leg[o, :, cut], preferred_element_type=F32)
            sums = terms[0 : 2 * keep] * shaping_ref[o, 0:1, cut]
            for f in range(1, nf):
                sums = sums + terms[f * 2 * keep : (f + 1) * 2 * keep] * shaping_ref[o, f : f + 1, cut]
            for t in range(width // LANES):
                for c in range(2):
                    row = (at // LANES + t) * 2 + c
                    stage[o, pl.ds(row, keep, stride=tiles2), :] = sums[
                        c * keep : (c + 1) * keep, t * LANES : (t + 1) * LANES
                    ]
        for b in range(keep):
            copy = pltpu.make_async_copy(
                stage.at[o, pl.ds(b * tiles2, tiles2)], out.at[b, o], out_sem.at[o, b]
            )
            copy.start()
            copies.append(copy)

    peers_order(lambda to: copy1(to).wait_send())
    peers_all(lambda f, o: copy2(f, o).wait_send())
    for copy in copies:
        copy.wait()


def on_device(nf, no, harmonics, legendre, beam_window, order_ids, noise_weight):
    maps, od, _, degrees = harmonics.shape
    _, lats, nlon = noise_weight.shape
    all_lats = legendre.shape[2]
    rows, half, total = no * od * 2, maps * 2, nf * no
    keep = maps // nf
    tiles = degrees // LANES
    leg = jnp.swapaxes(legendre, 1, 2)
    harm = harmonics.reshape(maps, od, 2, tiles, LANES)
    harm = jnp.swapaxes(harm, 2, 3).reshape(maps, od, tiles * 2, LANES)
    hbm = pl.BlockSpec(memory_space=pltpu.HBM)
    span = no * LANES
    ahead = rows * lats * span * 4 <= 8 * 2**20
    dma = pltpu.SemaphoreType.DMA
    out = pl.pallas_call(
        functools.partial(gather_kernel, nf, no),
        out_shape=jax.ShapeDtypeStruct((keep, od, tiles * 2, LANES), F32),
        in_specs=[hbm, hbm, hbm, hbm, hbm],
        out_specs=hbm,
        scratch_shapes=[
            pltpu.SMEM(order_ids.shape, jnp.int32),
            pltpu.VMEM(beam_window.shape, F32),
            pltpu.VMEM(harm.shape, BF16),
            pltpu.VMEM(leg.shape, BF16),
            pltpu.VMEM(noise_weight.shape, F32),
            pltpu.VMEM((od, maps * tiles * 2, LANES), F32),
            pltpu.VMEM((rows, nlon), F32),
            pltpu.VMEM((rows, nlon), BF16),
            pltpu.VMEM((rows * lats, rows), F32),
            pltpu.VMEM((rows * 2, span), BF16),
            pltpu.VMEM((rows * lats if ahead else 2 * od * lats, span), F32),
            pltpu.VMEM((no, lats, od * half), F32),
            pltpu.VMEM((no, lats, od * half), F32),
            pltpu.VMEM((nf, no, lats // nf, od * half), F32),
            pltpu.VMEM((nf, no, lats // nf, od * half), F32),
            pltpu.VMEM((nf, od * half, all_lats), F32),
            pltpu.VMEM((od, nf, degrees), F32),
            pltpu.VMEM((od, keep * tiles * 2, LANES), F32),
            dma((5,)),
            dma((no,)),
            dma((no,)),
            dma((total,)),
            dma((total,)),
            dma((od, keep)),
        ],
        compiler_params=pltpu.CompilerParams(
            collective_id=0, has_side_effects=True, vmem_limit_bytes=60 * 2**20
        ),
        name="operator",
    )(order_ids, beam_window, harm, leg, noise_weight)
    out = jnp.swapaxes(out.reshape(keep, od, tiles, 2, LANES), 2, 3)
    return out.reshape(keep, od, 2, degrees)


def solution(mesh):
    sizes = dict(mesh.shape)
    return jax.shard_map(
        functools.partial(on_device, sizes["freq"], sizes["order"]),
        mesh=mesh,
        in_specs=(
            P(None, "order", None, None),
            P("order", None, None),
            P(),
            P(),
            P("freq", "order", None),
        ),
        out_specs=P("freq", "order", None, None),
        check_vma=False,
    )
```

```python
import functools
import math

import jax
import jax.numpy as jnp
from jax import lax
from jax.experimental import pallas as pl
from jax.experimental.pallas import tpu as pltpu
from jax.sharding import PartitionSpec as P

MESH = pl.DeviceIdType.MESH
NT = (((1,), (1,)), ((), ()))
LANES = 128
F32 = jnp.float32
BF16 = jnp.bfloat16


def sin_cos_turns(step, period):
    turns = step.astype(F32) * (4.0 / period)
    quarter = jnp.floor(turns + 0.5)
    x = (turns - quarter) * (0.5 * math.pi)
    y = x * x
    sin = x * (1.0 + y * (-1.0 / 6 + y * (1.0 / 120 + y * (-1.0 / 5040 + y * (1.0 / 362880)))))
    cos = 1.0 + y * (-0.5 + y * (1.0 / 24 + y * (-1.0 / 720 + y * (1.0 / 40320 - y * (1.0 / 3628800)))))
    quad = quarter.astype(jnp.int32) & 3
    odd = (quad & 1) == 1
    c = jnp.where(odd, sin, cos)
    s = jnp.where(odd, cos, sin)
    c = jnp.where((quad == 1) | (quad == 2), -c, c)
    s = jnp.where(quad >= 2, -s, s)
    return c, s


def build_table(ids, wide, table, slots, nlon):
    shape = (slots, LANES)
    row = lax.broadcasted_iota(jnp.int32, shape, 0)
    lane = lax.broadcasted_iota(jnp.int32, shape, 1)
    order = jnp.zeros(shape, jnp.int32)
    for slot in range(slots):
        order = jnp.where(row >= slot, ids[slot], order)
    c, s = sin_cos_turns(lax.rem(order * lane, nlon), nlon)
    factor = jnp.where(order == 0, 1.0, 2.0).astype(F32)
    wide[0:slots, 0:LANES] = c * factor
    wide[slots : 2 * slots, 0:LANES] = -s * factor
    doublings = int(math.log2(nlon // LANES))
    reach = jnp.left_shift(LANES, jnp.minimum(lane, doublings))
    rc, rs = sin_cos_turns(lax.rem(order * reach, nlon), nlon)
    for level in range(doublings):
        bc = jnp.broadcast_to(rc[:, level : level + 1], shape)
        bs = jnp.broadcast_to(rs[:, level : level + 1], shape)
        for part in range(2**level):
            old = slice(part * LANES, (part + 1) * LANES)
            new = slice((part + 2**level) * LANES, (part + 1 + 2**level) * LANES)
            c, s = wide[0:slots, old], wide[slots : 2 * slots, old]
            wide[0:slots, new] = c * bc + s * bs
            wide[slots : 2 * slots, new] = s * bc - c * bs
    rounded = wide[...].astype(BF16)
    table[...] = rounded
    wide[...] = rounded.astype(F32)


def wrap(value, n):
    return jnp.where(value >= n, value - n, value)


def gather_kernel(
    nf, no, ids_hbm, beam_hbm, harm_hbm, leg_hbm, noise_hbm, out,
    ids, beam, harm, leg, noise, wide, table, gram, fan, spread, xs, xr, vs, vr, flipped,
    shaping_ref, stage, load_sem, send1, recv1, send2, recv2, out_sem,
):
    maps, od, tiles2, _ = harm.shape
    tiles = tiles2 // 2
    lats, nlon = noise.shape[1], noise.shape[2]
    all_lats = leg.shape[1]
    rows = no * od * 2
    half = maps * 2
    total = nf * no
    myf, me = lax.axis_index("freq"), lax.axis_index("order")
    lin = myf * no + me

    def peers_order(act):
        if no <= 16:
            for k in range(1, no):
                act(wrap(me + k, no))
        else:
            lax.fori_loop(1, no, lambda k, c: (act(wrap(me + k, no)), c)[1], 0)

    def peers_all(act):
        for g in range(nf):
            f = wrap(myf + g, nf)
            low = 1 if g == 0 else 0
            if total <= 64:
                for k in range(low, no):
                    act(f, wrap(me + k, no))
            else:
                lax.fori_loop(low, no, lambda k, c: (act(f, wrap(me + k, no)), c)[1], 0)

    loads = [
        pltpu.make_async_copy(ids_hbm, ids, load_sem.at[0]),
        pltpu.make_async_copy(harm_hbm, harm, load_sem.at[1]),
        pltpu.make_async_copy(beam_hbm, beam, load_sem.at[2]),
        pltpu.make_async_copy(leg_hbm, leg, load_sem.at[3]),
        pltpu.make_async_copy(noise_hbm, noise, load_sem.at[4]),
    ]
    for load in loads:
        load.start()

    barrier = pltpu.get_barrier_semaphore()

    def greet(f, o):
        pl.semaphore_signal(barrier, inc=1, device_id=(f, o), device_id_type=MESH)

    peers_all(greet)

    loads[0].wait()
    build_table(ids, wide, table, no * od, nlon)

    span = no * LANES
    p = lax.broadcasted_iota(jnp.int32, (rows, span), 0)
    q = lax.broadcasted_iota(jnp.int32, (rows, span), 1)
    begin = jnp.where(p < no * od, p * half, (p - no * od) * half + maps)
    fan_half = ((q >= begin) & (q < begin + maps)).astype(F32).astype(BF16)
    fan[...] = jnp.concatenate([fan_half, fan_half], axis=0)

    loads[2].wait()
    degrees = beam.shape[1]
    degree = lax.broadcasted_iota(jnp.int32, (1, degrees), 1)
    for o in range(od):
        shaping_ref[o] = jnp.where(degree >= ids[me * od + o], beam[...], 0.0)
    loads[1].wait()
    loads[3].wait()
    step = 8
    parts = []
    for o in range(od):
        shaping = shaping_ref[o, pl.ds(myf, 1), :]
        acc = jnp.zeros((all_lats, half), F32)
        for at in range(0, tiles, step):
            block = harm[:, o, 2 * at : 2 * (at + step), :].astype(F32)
            block = jnp.swapaxes(block, 0, 1)
            piece = jnp.concatenate(
                [
                    jnp.concatenate(
                        [
                            block[2 * t + c] * shaping[:, (at + t) * LANES : (at + t + 1) * LANES]
                            for t in range(step)
                        ],
                        axis=1,
                    )
                    for c in range(2)
                ],
                axis=0,
            ).astype(BF16)
            cut = slice(at * LANES, (at + step) * LANES)
            acc = acc + lax.dot_general(leg[o, :, cut], piece, NT, preferred_element_type=F32)
        parts.append(acc)
    columns = jnp.concatenate(parts, axis=1).astype(BF16).astype(F32)
    xs[...] = columns.reshape(no, lats, od * half)
    xr[me] = xs[me]

    pl.semaphore_wait(barrier, total - 1)

    def copy1(to):
        return pltpu.make_async_remote_copy(
            xs.at[to], xr.at[me], send1.at[to], recv1.at[me],
            device_id=(myf, to), device_id_type=MESH,
        )

    def arrive1(frm):
        pltpu.make_async_remote_copy(
            xs.at[frm], xr.at[frm], send1.at[frm], recv1.at[frm],
            device_id=(myf, frm), device_id_type=MESH,
        ).wait_recv()

    peers_order(lambda to: copy1(to).start())

    loads[4].wait()
    wide_step = 1024

    def gram_step(i, acc):
        cut = pl.ds(pl.multiple_of(i * wide_step, wide_step), wide_step)
        weight = noise[0, :, cut]
        left = [(wide[row : row + 1, cut] * weight) for row in range(rows)]
        left = jnp.concatenate(left, axis=0).astype(BF16)
        return acc + lax.dot_general(left, table[:, cut], NT, preferred_element_type=F32)

    ahead = spread.shape[0] == rows * lats
    acc = lax.fori_loop(
        0, nlon // wide_step, gram_step, jnp.zeros((rows * lats, rows), F32), unroll=ahead
    )
    gram[...] = acc * (1.0 / math.sqrt(2.0 * no * od) / math.sqrt(1.0 * nlon))

    def expand(value):
        high = value.astype(BF16)
        low = (value - high.astype(F32)).astype(BF16)
        both = jnp.concatenate([high, low], axis=1)
        return jnp.dot(both, fan[...], preferred_element_type=F32)

    if ahead:
        spread[...] = expand(gram[...])

    peers_order(arrive1)

    keep = maps // nf
    folds = lats // nf
    lane = lax.broadcasted_iota(jnp.int32, (lats, LANES), 1)
    sub = lax.broadcasted_iota(jnp.int32, (lats, LANES), 0)
    part = lane // maps
    slot = lax.rem(lane, maps) // keep
    own_slot = slot == lax.rem(sub, nf)

    def pack(d, value):
        turned = [value]
        for k in range(1, nf):
            turned.append(
                jnp.where(
                    slot >= k,
                    pltpu.roll(value, k * keep, 1),
                    pltpu.roll(value, LANES + k * keep - maps, 1),
                )
            )
        for f in range(nf):
            own = turned[-f % nf]
            for at in range(1, nf):
                own = jnp.where(slot == at, turned[(at - f) % nf], own)
            own = jnp.where(own_slot, own, 0.0)
            shift = 1
            while shift < nf:
                own = own + pltpu.roll(own, lats - shift, 0)
                shift *= 2
            for row in range(folds):
                vs[f, d, row : row + 1, :] = own[row * nf : row * nf + 1]

    def unpack(f, o):
        value = jnp.broadcast_to(vr[f, o, 0:1, :], (lats, LANES))
        for row in range(1, folds):
            value = jnp.where(sub >= row * nf, jnp.broadcast_to(vr[f, o, row : row + 1, :], (lats, LANES)), value)
        value = jnp.where(own_slot, value, 0.0)
        shift = 1
        while shift < nf:
            value = value + pltpu.roll(value, LANES - shift * keep, 1)
            shift *= 2
        return value

    def mix(d, get):
        out = None
        for s in range(2 * od):
            t = get(s, 0) * xr[0]
            for o in range(1, no):
                t = t + get(s, o) * xr[o]
            t = t + pltpu.roll(t, half, 1)
            t = t + pltpu.roll(t, maps, 1)
            out = t if out is None else jnp.where(part == s, t, out)
        pack(d, out.astype(BF16).astype(F32))

    group = od * lats
    if ahead:
        def early(d, s, o):
            at = ((s % 2) * no * od + d * od + s // 2) * lats
            return spread[at : at + lats, o * LANES : (o + 1) * LANES]
        for d in range(no):
            mix(d, functools.partial(early, d))
    else:
        def late(d, carry):
            for c in range(2):
                at = pl.multiple_of((c * no + d) * group, group)
                spread[c * group : (c + 1) * group] = expand(gram[pl.ds(at, group), :])
            def get(s, o):
                at = (s % 2) * group + s // 2 * lats
                return spread[at : at + lats, o * LANES : (o + 1) * LANES]
            mix(d, get)
            return carry
        lax.fori_loop(0, no, late, 0)

    vr[myf, me] = vs[myf, me]

    def copy2(f, o):
        return pltpu.make_async_remote_copy(
            vs.at[f, o], vr.at[myf, me], send2.at[f * no + o], recv2.at[lin],
            device_id=(f, o), device_id_type=MESH,
        )

    def arrive2(f, o):
        frm = f * no + o
        pltpu.make_async_remote_copy(
            vs.at[f, o], vr.at[f, o], send2.at[frm], recv2.at[frm],
            device_id=(f, o), device_id_type=MESH,
        ).wait_recv()

    peers_all(lambda f, o: copy2(f, o).start())
    peers_all(arrive2)

    for f in range(nf):
        flipped[f] = jnp.concatenate([unpack(f, o) for o in range(no)], axis=0).T

    width = 1024
    copies = []
    for o in range(od):
        pieces = []
        for f in range(nf):
            for c in range(2):
                at = o * half + c * maps
                pieces.append(flipped[f, at : at + keep, :])
        z = jnp.concatenate(pieces, axis=0).astype(BF16)
        for at in range(0, degrees, width):
            cut = slice(at, at + width)
            terms = jnp.dot(z, leg[o, :, cut], preferred_element_type=F32)
            sums = terms[0 : 2 * keep] * shaping_ref[o, 0:1, cut]
            for f in range(1, nf):
                sums = sums + terms[f * 2 * keep : (f + 1) * 2 * keep] * shaping_ref[o, f : f + 1, cut]
            for t in range(width // LANES):
                for c in range(2):
                    row = (at // LANES + t) * 2 + c
                    stage[o, pl.ds(row, keep, stride=tiles2), :] = sums[
                        c * keep : (c + 1) * keep, t * LANES : (t + 1) * LANES
                    ]

        for b in range(keep):
            copy = pltpu.make_async_copy(
                stage.at[o, pl.ds(b * tiles2, tiles2)], out.at[b, o], out_sem.at[o, b]
            )
            copy.start()
            copies.append(copy)

    peers_order(lambda to: copy1(to).wait_send())
    peers_all(lambda f, o: copy2(f, o).wait_send())
    for copy in copies:
        copy.wait()


def on_device(nf, no, harmonics, legendre, beam_window, order_ids, noise_weight):
    maps, od, _, degrees = harmonics.shape
    _, lats, nlon = noise_weight.shape
    all_lats = legendre.shape[2]
    rows, half, total = no * od * 2, maps * 2, nf * no
    keep = maps // nf
    tiles = degrees // LANES
    leg = jnp.swapaxes(legendre, 1, 2)
    harm = harmonics.reshape(maps, od, 2, tiles, LANES)
    harm = jnp.swapaxes(harm, 2, 3).reshape(maps, od, tiles * 2, LANES)
    hbm = pl.BlockSpec(memory_space=pltpu.HBM)
    span = no * LANES
    ahead = rows * lats * span * 4 <= 8 * 2**20
    dma = pltpu.SemaphoreType.DMA
    out = pl.pallas_call(
        functools.partial(gather_kernel, nf, no),
        out_shape=jax.ShapeDtypeStruct((keep, od, tiles * 2, LANES), F32),
        in_specs=[hbm, hbm, hbm, hbm, hbm],
        out_specs=hbm,
        scratch_shapes=[
            pltpu.SMEM(order_ids.shape, jnp.int32),
            pltpu.VMEM(beam_window.shape, F32),
            pltpu.VMEM(harm.shape, BF16),
            pltpu.VMEM(leg.shape, BF16),
            pltpu.VMEM(noise_weight.shape, F32),
            pltpu.VMEM((rows, nlon), F32),
            pltpu.VMEM((rows, nlon), BF16),
            pltpu.VMEM((rows * lats, rows), F32),
            pltpu.VMEM((rows * 2, span), BF16),
            pltpu.VMEM((rows * lats if ahead else 2 * od * lats, span), F32),
            pltpu.VMEM((no, lats, od * half), F32),
            pltpu.VMEM((no, lats, od * half), F32),
            pltpu.VMEM((nf, no, lats // nf, od * half), F32),
            pltpu.VMEM((nf, no, lats // nf, od * half), F32),
            pltpu.VMEM((nf, od * half, all_lats), F32),
            pltpu.VMEM((od, nf, degrees), F32),
            pltpu.VMEM((od, keep * tiles * 2, LANES), F32),
            dma((5,)),
            dma((no,)),
            dma((no,)),
            dma((total,)),
            dma((total,)),
            dma((od, keep)),
        ],
        compiler_params=pltpu.CompilerParams(
            collective_id=0, has_side_effects=True, vmem_limit_bytes=60 * 2**20
        ),
        name="operator",
    )(order_ids, beam_window, harm, leg, noise_weight)
    out = jnp.swapaxes(out.reshape(keep, od, tiles, 2, LANES), 2, 3)
    return out.reshape(keep, od, 2, degrees)


def solution(mesh):
    sizes = dict(mesh.shape)
    return jax.shard_map(
        functools.partial(on_device, sizes["freq"], sizes["order"]),
        mesh=mesh,
        in_specs=(
            P(None, "order", None, None),
            P("order", None, None),
            P(),
            P(),
            P("freq", "order", None),
        ),
        out_specs=P("freq", "order", None, None),
        check_vma=False,
    )
```

```python
import functools
import math

import jax
import jax.numpy as jnp
from jax import lax
from jax.experimental import pallas as pl
from jax.experimental.pallas import tpu as pltpu
from jax.sharding import PartitionSpec as P

MESH = pl.DeviceIdType.MESH
NT = (((1,), (1,)), ((), ()))
LANES = 128
F32 = jnp.float32
BF16 = jnp.bfloat16


def sin_cos_turns(step, period):
    turns = step.astype(F32) * (4.0 / period)
    quarter = jnp.floor(turns + 0.5)
    x = (turns - quarter) * (0.5 * math.pi)
    y = x * x
    sin = x * (1.0 + y * (-1.0 / 6 + y * (1.0 / 120 + y * (-1.0 / 5040 + y * (1.0 / 362880)))))
    cos = 1.0 + y * (-0.5 + y * (1.0 / 24 + y * (-1.0 / 720 + y * (1.0 / 40320 - y * (1.0 / 3628800)))))
    quad = quarter.astype(jnp.int32) & 3
    odd = (quad & 1) == 1
    c = jnp.where(odd, sin, cos)
    s = jnp.where(odd, cos, sin)
    c = jnp.where((quad == 1) | (quad == 2), -c, c)
    s = jnp.where(quad >= 2, -s, s)
    return c, s


def build_table(ids, wide, table, slots, nlon):
    shape = (slots, LANES)
    row = lax.broadcasted_iota(jnp.int32, shape, 0)
    lane = lax.broadcasted_iota(jnp.int32, shape, 1)
    order = jnp.zeros(shape, jnp.int32)
    for slot in range(slots):
        order = jnp.where(row >= slot, ids[slot], order)
    c, s = sin_cos_turns(lax.rem(order * lane, nlon), nlon)
    factor = jnp.where(order == 0, 1.0, 2.0).astype(F32)
    wide[0:slots, 0:LANES] = c * factor
    wide[slots : 2 * slots, 0:LANES] = -s * factor
    doublings = int(math.log2(nlon // LANES))
    reach = jnp.left_shift(LANES, jnp.minimum(lane, doublings))
    rc, rs = sin_cos_turns(lax.rem(order * reach, nlon), nlon)
    for level in range(doublings):
        bc = jnp.broadcast_to(rc[:, level : level + 1], shape)
        bs = jnp.broadcast_to(rs[:, level : level + 1], shape)
        for part in range(2**level):
            old = slice(part * LANES, (part + 1) * LANES)
            new = slice((part + 2**level) * LANES, (part + 1 + 2**level) * LANES)
            c, s = wide[0:slots, old], wide[slots : 2 * slots, old]
            wide[0:slots, new] = c * bc + s * bs
            wide[slots : 2 * slots, new] = s * bc - c * bs
    rounded = wide[...].astype(BF16)
    table[...] = rounded
    wide[...] = rounded.astype(F32)


def wrap(value, n):
    return jnp.where(value >= n, value - n, value)


def gather_kernel(
    nf, no, ids_hbm, beam_hbm, harm_hbm, leg_hbm, noise_hbm, out,
    ids, beam, harm, leg, noise, wide, table, gram, fan, spread, xs, xr, vs, vr, flipped,
    shaping_ref, stage, load_sem, send1, recv1, send2, recv2, out_sem,
):
    maps, od, tiles2, _ = harm.shape
    tiles = tiles2 // 2
    lats, nlon = noise.shape[1], noise.shape[2]
    all_lats = leg.shape[1]
    rows = no * od * 2
    half = maps * 2
    total = nf * no
    myf, me = lax.axis_index("freq"), lax.axis_index("order")
    lin = myf * no + me

    def peers_order(act):
        if no <= 16:
            for k in range(1, no):
                act(wrap(me + k, no))
        else:
            lax.fori_loop(1, no, lambda k, c: (act(wrap(me + k, no)), c)[1], 0)

    def peers_all(act):
        for g in range(nf):
            f = wrap(myf + g, nf)
            low = 1 if g == 0 else 0
            if total <= 64:
                for k in range(low, no):
                    act(f, wrap(me + k, no))
            else:
                lax.fori_loop(low, no, lambda k, c: (act(f, wrap(me + k, no)), c)[1], 0)

    loads = [
        pltpu.make_async_copy(ids_hbm, ids, load_sem.at[0]),
        pltpu.make_async_copy(harm_hbm, harm, load_sem.at[1]),
        pltpu.make_async_copy(beam_hbm, beam, load_sem.at[2]),
        pltpu.make_async_copy(leg_hbm, leg, load_sem.at[3]),
        pltpu.make_async_copy(noise_hbm, noise, load_sem.at[4]),
    ]
    for load in loads:
        load.start()

    barrier = pltpu.get_barrier_semaphore()

    def greet(f, o):
        pl.semaphore_signal(barrier, inc=1, device_id=(f, o), device_id_type=MESH)

    peers_all(greet)

    loads[0].wait()
    build_table(ids, wide, table, no * od, nlon)

    span = no * LANES
    p = lax.broadcasted_iota(jnp.int32, (rows, span), 0)
    q = lax.broadcasted_iota(jnp.int32, (rows, span), 1)
    begin = jnp.where(p < no * od, p * half, (p - no * od) * half + maps)
    fan_half = ((q >= begin) & (q < begin + maps)).astype(F32).astype(BF16)
    fan[...] = jnp.concatenate([fan_half, fan_half], axis=0)

    loads[2].wait()
    degrees = beam.shape[1]
    degree = lax.broadcasted_iota(jnp.int32, (1, degrees), 1)
    for o in range(od):
        shaping_ref[o] = jnp.where(degree >= ids[me * od + o], beam[...], 0.0)
    loads[1].wait()
    loads[3].wait()
    step = 8
    parts = []
    for o in range(od):
        shaping = shaping_ref[o, pl.ds(myf, 1), :]
        acc = jnp.zeros((all_lats, half), F32)
        for at in range(0, tiles, step):
            block = harm[:, o, 2 * at : 2 * (at + step), :].astype(F32)
            block = jnp.swapaxes(block, 0, 1)
            piece = jnp.concatenate(
                [
                    jnp.concatenate(
                        [
                            block[2 * t + c] * shaping[:, (at + t) * LANES : (at + t + 1) * LANES]
                            for t in range(step)
                        ],
                        axis=1,
                    )
                    for c in range(2)
                ],
                axis=0,
            ).astype(BF16)
            cut = slice(at * LANES, (at + step) * LANES)
            acc = acc + lax.dot_general(leg[o, :, cut], piece, NT, preferred_element_type=F32)
        parts.append(acc)
    columns = jnp.concatenate(parts, axis=1).astype(BF16).astype(F32)
    xs[...] = columns.reshape(no, lats, od * half)
    xr[me] = xs[me]

    pl.semaphore_wait(barrier, total - 1)

    def copy1(to):
        return pltpu.make_async_remote_copy(
            xs.at[to], xr.at[me], send1.at[to], recv1.at[me],
            device_id=(myf, to), device_id_type=MESH,
        )

    def arrive1(frm):
        pltpu.make_async_remote_copy(
            xs.at[frm], xr.at[frm], send1.at[frm], recv1.at[frm],
            device_id=(myf, frm), device_id_type=MESH,
        ).wait_recv()

    peers_order(lambda to: copy1(to).start())

    loads[4].wait()
    wide_step = 1024

    def gram_step(i, acc):
        cut = pl.ds(pl.multiple_of(i * wide_step, wide_step), wide_step)
        weight = noise[0, :, cut]
        left = [(wide[row : row + 1, cut] * weight) for row in range(rows)]
        left = jnp.concatenate(left, axis=0).astype(BF16)
        return acc + lax.dot_general(left, table[:, cut], NT, preferred_element_type=F32)

    ahead = spread.shape[0] == rows * lats
    acc = lax.fori_loop(
        0, nlon // wide_step, gram_step, jnp.zeros((rows * lats, rows), F32), unroll=ahead
    )
    gram[...] = acc * (1.0 / math.sqrt(2.0 * no * od) / math.sqrt(1.0 * nlon))

    def expand(value):
        high = value.astype(BF16)
        low = (value - high.astype(F32)).astype(BF16)
        both = jnp.concatenate([high, low], axis=1)
        return jnp.dot(both, fan[...], preferred_element_type=F32)

    if ahead:
        spread[...] = expand(gram[...])

    peers_order(arrive1)

    keep = maps // nf
    folds = lats // nf
    lane = lax.broadcasted_iota(jnp.int32, (lats, LANES), 1)
    sub = lax.broadcasted_iota(jnp.int32, (lats, LANES), 0)
    part = lane // maps
    slot = lax.rem(lane, maps) // keep
    own_slot = slot == lax.rem(sub, nf)

    def pack(d, value):
        turned = [value]
        for k in range(1, nf):
            turned.append(
                jnp.where(
                    slot >= k,
                    pltpu.roll(value, k * keep, 1),
                    pltpu.roll(value, LANES + k * keep - maps, 1),
                )
            )
        for f in range(nf):
            own = turned[-f % nf]
            for at in range(1, nf):
                own = jnp.where(slot == at, turned[(at - f) % nf], own)
            own = jnp.where(own_slot, own, 0.0)
            shift = 1
            while shift < nf:
                own = own + pltpu.roll(own, lats - shift, 0)
                shift *= 2
            for row in range(folds):
                vs[f, d, row : row + 1, :] = own[row * nf : row * nf + 1]

    def unpack(f, o):
        value = jnp.broadcast_to(vr[f, o, 0:1, :], (lats, LANES))
        for row in range(1, folds):
            value = jnp.where(sub >= row * nf, jnp.broadcast_to(vr[f, o, row : row + 1, :], (lats, LANES)), value)
        value = jnp.where(own_slot, value, 0.0)
        shift = 1
        while shift < nf:
            value = value + pltpu.roll(value, LANES - shift * keep, 1)
            shift *= 2
        return value

    def mix(d, get):
        out = None
        for s in range(2 * od):
            t = get(s, 0) * xr[0]
            for o in range(1, no):
                t = t + get(s, o) * xr[o]
            t = t + pltpu.roll(t, half, 1)
            t = t + pltpu.roll(t, maps, 1)
            out = t if out is None else jnp.where(part == s, t, out)
        pack(d, out.astype(BF16).astype(F32))

    def copy2(f, o):
        return pltpu.make_async_remote_copy(
            vs.at[f, o], vr.at[myf, me], send2.at[f * no + o], recv2.at[lin],
            device_id=(f, o), device_id_type=MESH,
        )

    group = od * lats

    def serve(d, own):
        if ahead:
            def get(s, o):
                at = pl.multiple_of((s % 2) * no * group + d * group + s // 2 * lats, lats)
                return spread[pl.ds(at, lats), o * LANES : (o + 1) * LANES]
        else:
            for c in range(2):
                at = pl.multiple_of((c * no + d) * group, group)
                spread[c * group : (c + 1) * group] = expand(gram[pl.ds(at, group), :])
            def get(s, o):
                at = (s % 2) * group + s // 2 * lats
                return spread[at : at + lats, o * LANES : (o + 1) * LANES]
        mix(d, get)
        for g in range(nf - 1 if own else nf):
            copy2(wrap(myf + g + 1, nf), d).start()

    if ahead:
        for k in range(1, no):
            serve(wrap(me + k, no), False)
    else:
        lax.fori_loop(1, no, lambda k, c: (serve(wrap(me + k, no), False), c)[1], 0)
    serve(me, True)
    vr[myf, me] = vs[myf, me]

    def arrive2(f, o):
        frm = f * no + o
        pltpu.make_async_remote_copy(
            vs.at[f, o], vr.at[f, o], send2.at[frm], recv2.at[frm],
            device_id=(f, o), device_id_type=MESH,
        ).wait_recv()

    peers_all(arrive2)

    for f in range(nf):
        flipped[f] = jnp.concatenate([unpack(f, o) for o in range(no)], axis=0).T

    width = 1024
    copies = []
    for o in range(od):
        pieces = []
        for f in range(nf):
            for c in range(2):
                at = o * half + c * maps
                pieces.append(flipped[f, at : at + keep, :])
        z = jnp.concatenate(pieces, axis=0).astype(BF16)
        for at in range(0, degrees, width):
            cut = slice(at, at + width)
            terms = jnp.dot(z, leg[o, :, cut], preferred_element_type=F32)
            sums = terms[0 : 2 * keep] * shaping_ref[o, 0:1, cut]
            for f in range(1, nf):
                sums = sums + terms[f * 2 * keep : (f + 1) * 2 * keep] * shaping_ref[o, f : f + 1, cut]
            for t in range(width // LANES):
                for c in range(2):
                    row = (at // LANES + t) * 2 + c
                    stage[o, pl.ds(row, keep, stride=tiles2), :] = sums[
                        c * keep : (c + 1) * keep, t * LANES : (t + 1) * LANES
                    ]

        for b in range(keep):
            copy = pltpu.make_async_copy(
                stage.at[o, pl.ds(b * tiles2, tiles2)], out.at[b, o], out_sem.at[o, b]
            )
            copy.start()
            copies.append(copy)

    peers_order(lambda to: copy1(to).wait_send())
    peers_all(lambda f, o: copy2(f, o).wait_send())
    for copy in copies:
        copy.wait()


def hand_over_kernel(source, out, sem):
    copies = [
        pltpu.make_async_copy(source.at[b], out.at[b], sem.at[b]) for b in range(source.shape[0])
    ]
    for copy in copies:
        copy.start()
    for copy in copies:
        copy.wait()


def on_device(nf, no, harmonics, legendre, beam_window, order_ids, noise_weight):
    maps, od, _, degrees = harmonics.shape
    _, lats, nlon = noise_weight.shape
    all_lats = legendre.shape[2]
    rows, half, total = no * od * 2, maps * 2, nf * no
    keep = maps // nf
    tiles = degrees // LANES
    leg = jnp.swapaxes(legendre, 1, 2)
    harm = harmonics.reshape(maps, od, 2, tiles, LANES)
    harm = jnp.swapaxes(harm, 2, 3).reshape(maps, od, tiles * 2, LANES)
    hbm = pl.BlockSpec(memory_space=pltpu.HBM)
    span = no * LANES
    ahead = rows * lats * span * 4 <= 8 * 2**20
    dma = pltpu.SemaphoreType.DMA
    out = pl.pallas_call(
        functools.partial(gather_kernel, nf, no),
        out_shape=jax.ShapeDtypeStruct((keep, od, tiles * 2, LANES), F32),
        in_specs=[hbm, hbm, hbm, hbm, hbm],
        out_specs=hbm,
        scratch_shapes=[
            pltpu.SMEM(order_ids.shape, jnp.int32),
            pltpu.VMEM(beam_window.shape, F32),
            pltpu.VMEM(harm.shape, BF16),
            pltpu.VMEM(leg.shape, BF16),
            pltpu.VMEM(noise_weight.shape, F32),
            pltpu.VMEM((rows, nlon), F32),
            pltpu.VMEM((rows, nlon), BF16),
            pltpu.VMEM((rows * lats, rows), F32),
            pltpu.VMEM((rows * 2, span), BF16),
            pltpu.VMEM((rows * lats if ahead else 2 * od * lats, span), F32),
            pltpu.VMEM((no, lats, od * half), F32),
            pltpu.VMEM((no, lats, od * half), F32),
            pltpu.VMEM((nf, no, lats // nf, od * half), F32),
            pltpu.VMEM((nf, no, lats // nf, od * half), F32),
            pltpu.VMEM((nf, od * half, all_lats), F32),
            pltpu.VMEM((od, nf, degrees), F32),
            pltpu.VMEM((od, keep * tiles * 2, LANES), F32),
            dma((5,)),
            dma((no,)),
            dma((no,)),
            dma((total,)),
            dma((total,)),
            dma((od, keep)),
        ],
        compiler_params=pltpu.CompilerParams(
            collective_id=0, has_side_effects=True, vmem_limit_bytes=60 * 2**20
        ),
        name="operator",
    )(order_ids, beam_window, harm, leg, noise_weight)
    out = pl.pallas_call(
        hand_over_kernel,
        out_shape=jax.ShapeDtypeStruct(out.shape, out.dtype),
        in_specs=[hbm],
        out_specs=hbm,
        scratch_shapes=[dma((keep,))],
        compiler_params=pltpu.CompilerParams(vmem_limit_bytes=60 * 2**20),
        name="hand_over",
    )(out)
    out = jnp.swapaxes(out.reshape(keep, od, tiles, 2, LANES), 2, 3)
    return out.reshape(keep, od, 2, degrees)


def solution(mesh):
    sizes = dict(mesh.shape)
    return jax.shard_map(
        functools.partial(on_device, sizes["freq"], sizes["order"]),
        mesh=mesh,
        in_specs=(
            P(None, "order", None, None),
            P("order", None, None),
            P(),
            P(),
            P("freq", "order", None),
        ),
        out_specs=P("freq", "order", None, None),
        check_vma=False,
    )
```

```python
import functools
import math

import jax
import jax.numpy as jnp
from jax import lax
from jax.experimental import pallas as pl
from jax.experimental.pallas import tpu as pltpu
from jax.sharding import PartitionSpec as P

MESH = pl.DeviceIdType.MESH
NT = (((1,), (1,)), ((), ()))
LANES = 128
F32 = jnp.float32
BF16 = jnp.bfloat16


def sin_cos_turns(step, period):
    turns = step.astype(F32) * (4.0 / period)
    quarter = jnp.floor(turns + 0.5)
    x = (turns - quarter) * (0.5 * math.pi)
    y = x * x
    sin = x * (1.0 + y * (-1.0 / 6 + y * (1.0 / 120 + y * (-1.0 / 5040 + y * (1.0 / 362880)))))
    cos = 1.0 + y * (-0.5 + y * (1.0 / 24 + y * (-1.0 / 720 + y * (1.0 / 40320 - y * (1.0 / 3628800)))))
    quad = quarter.astype(jnp.int32) & 3
    odd = (quad & 1) == 1
    c = jnp.where(odd, sin, cos)
    s = jnp.where(odd, cos, sin)
    c = jnp.where((quad == 1) | (quad == 2), -c, c)
    s = jnp.where(quad >= 2, -s, s)
    return c, s


def build_table(ids, wide, table, slots, nlon):
    shape = (slots, LANES)
    row = lax.broadcasted_iota(jnp.int32, shape, 0)
    lane = lax.broadcasted_iota(jnp.int32, shape, 1)
    order = jnp.zeros(shape, jnp.int32)
    for slot in range(slots):
        order = jnp.where(row >= slot, ids[slot], order)
    c, s = sin_cos_turns(lax.rem(order * lane, nlon), nlon)
    factor = jnp.where(order == 0, 1.0, 2.0).astype(F32)
    wide[0:slots, 0:LANES] = c * factor
    wide[slots : 2 * slots, 0:LANES] = -s * factor
    doublings = int(math.log2(nlon // LANES))
    reach = jnp.left_shift(LANES, jnp.minimum(lane, doublings))
    rc, rs = sin_cos_turns(lax.rem(order * reach, nlon), nlon)
    for level in range(doublings):
        bc = jnp.broadcast_to(rc[:, level : level + 1], shape)
        bs = jnp.broadcast_to(rs[:, level : level + 1], shape)
        for part in range(2**level):
            old = slice(part * LANES, (part + 1) * LANES)
            new = slice((part + 2**level) * LANES, (part + 1 + 2**level) * LANES)
            c, s = wide[0:slots, old], wide[slots : 2 * slots, old]
            wide[0:slots, new] = c * bc + s * bs
            wide[slots : 2 * slots, new] = s * bc - c * bs
    rounded = wide[...].astype(BF16)
    table[...] = rounded
    wide[...] = rounded.astype(F32)


def wrap(value, n):
    return jnp.where(value >= n, value - n, value)


def gather_kernel(
    nf, no, ids_hbm, beam_hbm, harm_hbm, leg_hbm, noise_hbm, out,
    ids, beam, harm, leg, noise, wide, table, gram, fan, spread, xs, xr, vs, vr, flipped,
    shaping_ref, stage, load_sem, send1, recv1, send2, recv2, out_sem,
):
    maps, od, tiles2, _ = harm.shape
    tiles = tiles2 // 2
    lats, nlon = noise.shape[1], noise.shape[2]
    all_lats = leg.shape[1]
    rows = no * od * 2
    half = maps * 2
    total = nf * no
    myf, me = lax.axis_index("freq"), lax.axis_index("order")
    lin = myf * no + me

    def peers_order(act):
        if no <= 16:
            for k in range(1, no):
                act(wrap(me + k, no))
        else:
            lax.fori_loop(1, no, lambda k, c: (act(wrap(me + k, no)), c)[1], 0)

    def peers_all(act):
        for g in range(nf):
            f = wrap(myf + g, nf)
            low = 1 if g == 0 else 0
            if total <= 64:
                for k in range(low, no):
                    act(f, wrap(me + k, no))
            else:
                lax.fori_loop(low, no, lambda k, c: (act(f, wrap(me + k, no)), c)[1], 0)

    loads = [
        pltpu.make_async_copy(ids_hbm, ids, load_sem.at[0]),
        pltpu.make_async_copy(harm_hbm, harm, load_sem.at[1]),
        pltpu.make_async_copy(beam_hbm, beam, load_sem.at[2]),
        pltpu.make_async_copy(leg_hbm, leg, load_sem.at[3]),
        pltpu.make_async_copy(noise_hbm, noise, load_sem.at[4]),
    ]
    for load in loads:
        load.start()

    barrier = pltpu.get_barrier_semaphore()

    def greet(f, o):
        pl.semaphore_signal(barrier, inc=1, device_id=(f, o), device_id_type=MESH)

    peers_all(greet)

    loads[0].wait()
    build_table(ids, wide, table, no * od, nlon)

    span = no * LANES
    p = lax.broadcasted_iota(jnp.int32, (rows, span), 0)
    q = lax.broadcasted_iota(jnp.int32, (rows, span), 1)
    begin = jnp.where(p < no * od, p * half, (p - no * od) * half + maps)
    fan_half = ((q >= begin) & (q < begin + maps)).astype(F32).astype(BF16)
    fan[...] = jnp.concatenate([fan_half, fan_half], axis=0)

    loads[2].wait()
    degrees = beam.shape[1]
    degree = lax.broadcasted_iota(jnp.int32, (1, degrees), 1)
    for o in range(od):
        shaping_ref[o] = jnp.where(degree >= ids[me * od + o], beam[...], 0.0)
    loads[1].wait()
    loads[3].wait()
    step = 8
    parts = []
    for o in range(od):
        shaping = shaping_ref[o, pl.ds(myf, 1), :]
        acc = jnp.zeros((all_lats, half), F32)
        for at in range(0, tiles, step):
            block = harm[:, o, 2 * at : 2 * (at + step), :].astype(F32)
            block = jnp.swapaxes(block, 0, 1)
            piece = jnp.concatenate(
                [
                    jnp.concatenate(
                        [
                            block[2 * t + c] * shaping[:, (at + t) * LANES : (at + t + 1) * LANES]
                            for t in range(step)
                        ],
                        axis=1,
                    )
                    for c in range(2)
                ],
                axis=0,
            ).astype(BF16)
            cut = slice(at * LANES, (at + step) * LANES)
            acc = acc + lax.dot_general(leg[o, :, cut], piece, NT, preferred_element_type=F32)
        parts.append(acc)
    columns = jnp.concatenate(parts, axis=1).astype(BF16).astype(F32)
    xs[...] = columns.reshape(no, lats, od * half)
    xr[me] = xs[me]

    pl.semaphore_wait(barrier, total - 1)

    def copy1(to):
        return pltpu.make_async_remote_copy(
            xs.at[to], xr.at[me], send1.at[to], recv1.at[me],
            device_id=(myf, to), device_id_type=MESH,
        )

    def arrive1(frm):
        pltpu.make_async_remote_copy(
            xs.at[frm], xr.at[frm], send1.at[frm], recv1.at[frm],
            device_id=(myf, frm), device_id_type=MESH,
        ).wait_recv()

    peers_order(lambda to: copy1(to).start())

    loads[4].wait()
    wide_step = 1024

    def gram_step(i, acc):
        cut = pl.ds(pl.multiple_of(i * wide_step, wide_step), wide_step)
        weight = noise[0, :, cut]
        left = [(wide[row : row + 1, cut] * weight) for row in range(rows)]
        left = jnp.concatenate(left, axis=0).astype(BF16)
        return acc + lax.dot_general(left, table[:, cut], NT, preferred_element_type=F32)

    ahead = spread.shape[0] == rows * lats
    acc = lax.fori_loop(
        0, nlon // wide_step, gram_step, jnp.zeros((rows * lats, rows), F32), unroll=ahead
    )
    gram[...] = acc * (1.0 / math.sqrt(2.0 * no * od) / math.sqrt(1.0 * nlon))

    def expand(value):
        high = value.astype(BF16)
        low = (value - high.astype(F32)).astype(BF16)
        both = jnp.concatenate([high, low], axis=1)
        return jnp.dot(both, fan[...], preferred_element_type=F32)

    if ahead:
        spread[...] = expand(gram[...])

    peers_order(arrive1)

    keep = maps // nf
    folds = lats // nf
    lane = lax.broadcasted_iota(jnp.int32, (lats, LANES), 1)
    sub = lax.broadcasted_iota(jnp.int32, (lats, LANES), 0)
    part = lane // maps
    slot = lax.rem(lane, maps) // keep
    own_slot = slot == lax.rem(sub, nf)

    def pack(d, value):
        turned = [value]
        for k in range(1, nf):
            turned.append(
                jnp.where(
                    slot >= k,
                    pltpu.roll(value, k * keep, 1),
                    pltpu.roll(value, LANES + k * keep - maps, 1),
                )
            )
        for f in range(nf):
            own = turned[-f % nf]
            for at in range(1, nf):
                own = jnp.where(slot == at, turned[(at - f) % nf], own)
            own = jnp.where(own_slot, own, 0.0)
            shift = 1
            while shift < nf:
                own = own + pltpu.roll(own, lats - shift, 0)
                shift *= 2
            for row in range(folds):
                vs[f, d, row : row + 1, :] = own[row * nf : row * nf + 1]

    def unpack(f, o):
        value = jnp.broadcast_to(vr[f, o, 0:1, :], (lats, LANES))
        for row in range(1, folds):
            value = jnp.where(sub >= row * nf, jnp.broadcast_to(vr[f, o, row : row + 1, :], (lats, LANES)), value)
        value = jnp.where(own_slot, value, 0.0)
        shift = 1
        while shift < nf:
            value = value + pltpu.roll(value, LANES - shift * keep, 1)
            shift *= 2
        return value

    def mix(d, get):
        out = None
        for s in range(2 * od):
            t = get(s, 0) * xr[0]
            for o in range(1, no):
                t = t + get(s, o) * xr[o]
            t = t + pltpu.roll(t, half, 1)
            t = t + pltpu.roll(t, maps, 1)
            out = t if out is None else jnp.where(part == s, t, out)
        pack(d, out.astype(BF16).astype(F32))

    group = od * lats
    if ahead:
        def early(d, s, o):
            at = ((s % 2) * no * od + d * od + s // 2) * lats
            return spread[at : at + lats, o * LANES : (o + 1) * LANES]
        for d in range(no):
            mix(d, functools.partial(early, d))
    else:
        def late(d, carry):
            for c in range(2):
                at = pl.multiple_of((c * no + d) * group, group)
                spread[c * group : (c + 1) * group] = expand(gram[pl.ds(at, group), :])
            def get(s, o):
                at = (s % 2) * group + s // 2 * lats
                return spread[at : at + lats, o * LANES : (o + 1) * LANES]
            mix(d, get)
            return carry
        lax.fori_loop(0, no, late, 0)

    vr[myf, me] = vs[myf, me]

    def copy2(f, o):
        return pltpu.make_async_remote_copy(
            vs.at[f, o], vr.at[myf, me], send2.at[f * no + o], recv2.at[lin],
            device_id=(f, o), device_id_type=MESH,
        )

    def arrive2(f, o):
        frm = f * no + o
        pltpu.make_async_remote_copy(
            vs.at[f, o], vr.at[f, o], send2.at[frm], recv2.at[frm],
            device_id=(f, o), device_id_type=MESH,
        ).wait_recv()

    peers_all(lambda f, o: copy2(f, o).start())
    peers_all(arrive2)

    for f in range(nf):
        flipped[f] = jnp.concatenate([unpack(f, o) for o in range(no)], axis=0).T

    width = 1024
    copies = []
    for o in range(od):
        pieces = []
        for f in range(nf):
            for c in range(2):
                at = o * half + c * maps
                pieces.append(flipped[f, at : at + keep, :])
        z = jnp.concatenate(pieces, axis=0).astype(BF16)
        for at in range(0, degrees, width):
            cut = slice(at, at + width)
            terms = jnp.dot(z, leg[o, :, cut], preferred_element_type=F32)
            sums = terms[0 : 2 * keep] * shaping_ref[o, 0:1, cut]
            for f in range(1, nf):
                sums = sums + terms[f * 2 * keep : (f + 1) * 2 * keep] * shaping_ref[o, f : f + 1, cut]
            for t in range(width // LANES):
                for c in range(2):
                    row = (at // LANES + t) * 2 + c
                    stage[o, pl.ds(row, keep, stride=tiles2), :] = sums[
                        c * keep : (c + 1) * keep, t * LANES : (t + 1) * LANES
                    ]

        for b in range(keep):
            copy = pltpu.make_async_copy(
                stage.at[o, pl.ds(b * tiles2, tiles2)], out.at[b, o], out_sem.at[o, b]
            )
            copy.start()
            copies.append(copy)

    peers_order(lambda to: copy1(to).wait_send())
    peers_all(lambda f, o: copy2(f, o).wait_send())
    for copy in copies:
        copy.wait()


def hand_over_kernel(source, out, held, sem_in, sem_out):
    keep = source.shape[0]
    fetch = [pltpu.make_async_copy(source.at[b], held.at[b], sem_in.at[b]) for b in range(keep)]
    store = [pltpu.make_async_copy(held.at[b], out.at[b], sem_out.at[b]) for b in range(keep)]
    for copy in fetch:
        copy.start()
    for b in range(keep):
        fetch[b].wait()
        store[b].start()
    for copy in store:
        copy.wait()


def on_device(nf, no, harmonics, legendre, beam_window, order_ids, noise_weight):
    maps, od, _, degrees = harmonics.shape
    _, lats, nlon = noise_weight.shape
    all_lats = legendre.shape[2]
    rows, half, total = no * od * 2, maps * 2, nf * no
    keep = maps // nf
    tiles = degrees // LANES
    leg = jnp.swapaxes(legendre, 1, 2)
    harm = harmonics.reshape(maps, od, 2, tiles, LANES)
    harm = jnp.swapaxes(harm, 2, 3).reshape(maps, od, tiles * 2, LANES)
    hbm = pl.BlockSpec(memory_space=pltpu.HBM)
    span = no * LANES
    ahead = rows * lats * span * 4 <= 8 * 2**20
    dma = pltpu.SemaphoreType.DMA
    out = pl.pallas_call(
        functools.partial(gather_kernel, nf, no),
        out_shape=jax.ShapeDtypeStruct((keep, od, tiles * 2, LANES), F32),
        in_specs=[hbm, hbm, hbm, hbm, hbm],
        out_specs=hbm,
        scratch_shapes=[
            pltpu.SMEM(order_ids.shape, jnp.int32),
            pltpu.VMEM(beam_window.shape, F32),
            pltpu.VMEM(harm.shape, BF16),
            pltpu.VMEM(leg.shape, BF16),
            pltpu.VMEM(noise_weight.shape, F32),
            pltpu.VMEM((rows, nlon), F32),
            pltpu.VMEM((rows, nlon), BF16),
            pltpu.VMEM((rows * lats, rows), F32),
            pltpu.VMEM((rows * 2, span), BF16),
            pltpu.VMEM((rows * lats if ahead else 2 * od * lats, span), F32),
            pltpu.VMEM((no, lats, od * half), F32),
            pltpu.VMEM((no, lats, od * half), F32),
            pltpu.VMEM((nf, no, lats // nf, od * half), F32),
            pltpu.VMEM((nf, no, lats // nf, od * half), F32),
            pltpu.VMEM((nf, od * half, all_lats), F32),
            pltpu.VMEM((od, nf, degrees), F32),
            pltpu.VMEM((od, keep * tiles * 2, LANES), F32),
            dma((5,)),
            dma((no,)),
            dma((no,)),
            dma((total,)),
            dma((total,)),
            dma((od, keep)),
        ],
        compiler_params=pltpu.CompilerParams(
            collective_id=0, has_side_effects=True, vmem_limit_bytes=60 * 2**20
        ),
        name="operator",
    )(order_ids, beam_window, harm, leg, noise_weight)
    out = pl.pallas_call(
        hand_over_kernel,
        out_shape=jax.ShapeDtypeStruct(out.shape, out.dtype),
        in_specs=[hbm],
        out_specs=hbm,
        scratch_shapes=[pltpu.VMEM(out.shape, F32), dma((keep,)), dma((keep,))],
        compiler_params=pltpu.CompilerParams(vmem_limit_bytes=60 * 2**20),
        name="hand_over",
    )(out)
    out = jnp.swapaxes(out.reshape(keep, od, tiles, 2, LANES), 2, 3)
    return out.reshape(keep, od, 2, degrees)


def solution(mesh):
    sizes = dict(mesh.shape)
    return jax.shard_map(
        functools.partial(on_device, sizes["freq"], sizes["order"]),
        mesh=mesh,
        in_specs=(
            P(None, "order", None, None),
            P("order", None, None),
            P(),
            P(),
            P("freq", "order", None),
        ),
        out_specs=P("freq", "order", None, None),
        check_vma=False,
    )
```

```python
import functools
import math

import jax
import jax.numpy as jnp
from jax import lax
from jax.experimental import pallas as pl
from jax.experimental.pallas import tpu as pltpu
from jax.sharding import PartitionSpec as P

MESH = pl.DeviceIdType.MESH
NT = (((1,), (1,)), ((), ()))
LANES = 128
F32 = jnp.float32
BF16 = jnp.bfloat16


def sin_cos_turns(step, period):
    turns = step.astype(F32) * (4.0 / period)
    quarter = jnp.floor(turns + 0.5)
    x = (turns - quarter) * (0.5 * math.pi)
    y = x * x
    sin = x * (1.0 + y * (-1.0 / 6 + y * (1.0 / 120 + y * (-1.0 / 5040 + y * (1.0 / 362880)))))
    cos = 1.0 + y * (-0.5 + y * (1.0 / 24 + y * (-1.0 / 720 + y * (1.0 / 40320 - y * (1.0 / 3628800)))))
    quad = quarter.astype(jnp.int32) & 3
    odd = (quad & 1) == 1
    c = jnp.where(odd, sin, cos)
    s = jnp.where(odd, cos, sin)
    c = jnp.where((quad == 1) | (quad == 2), -c, c)
    s = jnp.where(quad >= 2, -s, s)
    return c, s


def build_table(ids, wide, table, slots, nlon):
    shape = (slots, LANES)
    row = lax.broadcasted_iota(jnp.int32, shape, 0)
    lane = lax.broadcasted_iota(jnp.int32, shape, 1)
    order = jnp.zeros(shape, jnp.int32)
    for slot in range(slots):
        order = jnp.where(row >= slot, ids[slot], order)
    c, s = sin_cos_turns(lax.rem(order * lane, nlon), nlon)
    factor = jnp.where(order == 0, 1.0, 2.0).astype(F32)
    wide[0:slots, 0:LANES] = c * factor
    wide[slots : 2 * slots, 0:LANES] = -s * factor
    doublings = int(math.log2(nlon // LANES))
    reach = jnp.left_shift(LANES, jnp.minimum(lane, doublings))
    rc, rs = sin_cos_turns(lax.rem(order * reach, nlon), nlon)
    for level in range(doublings):
        bc = jnp.broadcast_to(rc[:, level : level + 1], shape)
        bs = jnp.broadcast_to(rs[:, level : level + 1], shape)
        for part in range(2**level):
            old = slice(part * LANES, (part + 1) * LANES)
            new = slice((part + 2**level) * LANES, (part + 1 + 2**level) * LANES)
            c, s = wide[0:slots, old], wide[slots : 2 * slots, old]
            wide[0:slots, new] = c * bc + s * bs
            wide[slots : 2 * slots, new] = s * bc - c * bs
    rounded = wide[...].astype(BF16)
    table[...] = rounded
    wide[...] = rounded.astype(F32)


def wrap(value, n):
    return jnp.where(value >= n, value - n, value)


def gather_kernel(
    nf, no, ids_hbm, beam_hbm, harm_hbm, leg_hbm, noise_hbm, out,
    ids, beam, harm, leg, noise, wide, table, gram, fan, spread, xs, xr, vs, vr, flipped,
    shaping_ref, stage, load_sem, send1, recv1, send2, recv2, out_sem,
):
    maps, od, tiles2, _ = harm.shape
    tiles = tiles2 // 2
    lats, nlon = noise.shape[1], noise.shape[2]
    all_lats = leg.shape[1]
    rows = no * od * 2
    half = maps * 2
    total = nf * no
    myf, me = lax.axis_index("freq"), lax.axis_index("order")
    lin = myf * no + me

    def peers_order(act):
        if no <= 16:
            for k in range(1, no):
                act(wrap(me + k, no))
        else:
            lax.fori_loop(1, no, lambda k, c: (act(wrap(me + k, no)), c)[1], 0)

    def peers_all(act):
        for g in range(nf):
            f = wrap(myf + g, nf)
            low = 1 if g == 0 else 0
            if total <= 64:
                for k in range(low, no):
                    act(f, wrap(me + k, no))
            else:
                lax.fori_loop(low, no, lambda k, c: (act(f, wrap(me + k, no)), c)[1], 0)

    loads = [
        pltpu.make_async_copy(ids_hbm, ids, load_sem.at[0]),
        pltpu.make_async_copy(harm_hbm, harm, load_sem.at[1]),
        pltpu.make_async_copy(beam_hbm, beam, load_sem.at[2]),
        pltpu.make_async_copy(leg_hbm, leg, load_sem.at[3]),
        pltpu.make_async_copy(noise_hbm, noise, load_sem.at[4]),
    ]
    for load in loads:
        load.start()

    barrier = pltpu.get_barrier_semaphore()

    def greet(f, o):
        pl.semaphore_signal(barrier, inc=1, device_id=(f, o), device_id_type=MESH)

    peers_all(greet)

    loads[0].wait()
    build_table(ids, wide, table, no * od, nlon)

    span = no * LANES
    p = lax.broadcasted_iota(jnp.int32, (rows, span), 0)
    q = lax.broadcasted_iota(jnp.int32, (rows, span), 1)
    begin = jnp.where(p < no * od, p * half, (p - no * od) * half + maps)
    fan_half = ((q >= begin) & (q < begin + maps)).astype(F32).astype(BF16)
    fan[...] = jnp.concatenate([fan_half, fan_half], axis=0)

    loads[2].wait()
    degrees = beam.shape[1]
    degree = lax.broadcasted_iota(jnp.int32, (1, degrees), 1)
    for o in range(od):
        shaping_ref[o] = jnp.where(degree >= ids[me * od + o], beam[...], 0.0)
    loads[1].wait()
    loads[3].wait()
    step = 8
    parts = []
    for o in range(od):
        shaping = shaping_ref[o, pl.ds(myf, 1), :]
        acc = jnp.zeros((all_lats, half), F32)
        for at in range(0, tiles, step):
            block = harm[:, o, 2 * at : 2 * (at + step), :].astype(F32)
            block = jnp.swapaxes(block, 0, 1)
            piece = jnp.concatenate(
                [
                    jnp.concatenate(
                        [
                            block[2 * t + c] * shaping[:, (at + t) * LANES : (at + t + 1) * LANES]
                            for t in range(step)
                        ],
                        axis=1,
                    )
                    for c in range(2)
                ],
                axis=0,
            ).astype(BF16)
            cut = slice(at * LANES, (at + step) * LANES)
            acc = acc + lax.dot_general(leg[o, :, cut], piece, NT, preferred_element_type=F32)
        parts.append(acc)
    columns = jnp.concatenate(parts, axis=1).astype(BF16).astype(F32)
    xs[...] = columns.reshape(no, lats, od * half)
    xr[me] = xs[me]

    pl.semaphore_wait(barrier, total - 1)

    def copy1(to):
        return pltpu.make_async_remote_copy(
            xs.at[to], xr.at[me], send1.at[to], recv1.at[me],
            device_id=(myf, to), device_id_type=MESH,
        )

    def arrive1(frm):
        pltpu.make_async_remote_copy(
            xs.at[frm], xr.at[frm], send1.at[frm], recv1.at[frm],
            device_id=(myf, frm), device_id_type=MESH,
        ).wait_recv()

    peers_order(lambda to: copy1(to).start())

    loads[4].wait()
    wide_step = 1024

    def gram_step(i, acc):
        cut = pl.ds(pl.multiple_of(i * wide_step, wide_step), wide_step)
        weight = noise[0, :, cut]
        left = [(wide[row : row + 1, cut] * weight) for row in range(rows)]
        left = jnp.concatenate(left, axis=0).astype(BF16)
        return acc + lax.dot_general(left, table[:, cut], NT, preferred_element_type=F32)

    ahead = spread.shape[0] == rows * lats
    acc = lax.fori_loop(
        0, nlon // wide_step, gram_step, jnp.zeros((rows * lats, rows), F32), unroll=ahead
    )
    gram[...] = acc * (1.0 / math.sqrt(2.0 * no * od) / math.sqrt(1.0 * nlon))

    def expand(value):
        high = value.astype(BF16)
        low = (value - high.astype(F32)).astype(BF16)
        both = jnp.concatenate([high, low], axis=1)
        return jnp.dot(both, fan[...], preferred_element_type=F32)

    if ahead:
        spread[...] = expand(gram[...])

    peers_order(arrive1)

    keep = maps // nf
    folds = lats // nf
    lane = lax.broadcasted_iota(jnp.int32, (lats, LANES), 1)
    sub = lax.broadcasted_iota(jnp.int32, (lats, LANES), 0)
    part = lane // maps
    slot = lax.rem(lane, maps) // keep
    own_slot = slot == lax.rem(sub, nf)

    def pack(d, value):
        turned = [value]
        for k in range(1, nf):
            turned.append(
                jnp.where(
                    slot >= k,
                    pltpu.roll(value, k * keep, 1),
                    pltpu.roll(value, LANES + k * keep - maps, 1),
                )
            )
        for f in range(nf):
            own = turned[-f % nf]
            for at in range(1, nf):
                own = jnp.where(slot == at, turned[(at - f) % nf], own)
            own = jnp.where(own_slot, own, 0.0)
            shift = 1
            while shift < nf:
                own = own + pltpu.roll(own, lats - shift, 0)
                shift *= 2
            for row in range(folds):
                vs[f, d, row : row + 1, :] = own[row * nf : row * nf + 1]

    def unpack(f, o):
        value = jnp.broadcast_to(vr[f, o, 0:1, :], (lats, LANES))
        for row in range(1, folds):
            value = jnp.where(sub >= row * nf, jnp.broadcast_to(vr[f, o, row : row + 1, :], (lats, LANES)), value)
        value = jnp.where(own_slot, value, 0.0)
        shift = 1
        while shift < nf:
            value = value + pltpu.roll(value, LANES - shift * keep, 1)
            shift *= 2
        return value

    def mix(d, get):
        out = None
        for s in range(2 * od):
            t = get(s, 0) * xr[0]
            for o in range(1, no):
                t = t + get(s, o) * xr[o]
            t = t + pltpu.roll(t, half, 1)
            t = t + pltpu.roll(t, maps, 1)
            out = t if out is None else jnp.where(part == s, t, out)
        pack(d, out.astype(BF16).astype(F32))

    group = od * lats
    if ahead:
        def early(d, s, o):
            at = ((s % 2) * no * od + d * od + s // 2) * lats
            return spread[at : at + lats, o * LANES : (o + 1) * LANES]
        for d in range(no):
            mix(d, functools.partial(early, d))
    else:
        def late(d, carry):
            for c in range(2):
                at = pl.multiple_of((c * no + d) * group, group)
                spread[c * group : (c + 1) * group] = expand(gram[pl.ds(at, group), :])
            def get(s, o):
                at = (s % 2) * group + s // 2 * lats
                return spread[at : at + lats, o * LANES : (o + 1) * LANES]
            mix(d, get)
            return carry
        lax.fori_loop(0, no, late, 0)

    vr[myf, me] = vs[myf, me]

    def copy2(f, o):
        return pltpu.make_async_remote_copy(
            vs.at[f, o], vr.at[myf, me], send2.at[f * no + o], recv2.at[lin],
            device_id=(f, o), device_id_type=MESH,
        )

    def arrive2(f, o):
        frm = f * no + o
        pltpu.make_async_remote_copy(
            vs.at[f, o], vr.at[f, o], send2.at[frm], recv2.at[frm],
            device_id=(f, o), device_id_type=MESH,
        ).wait_recv()

    peers_all(lambda f, o: copy2(f, o).start())

    for g in range(nf):
        f = wrap(myf + g, nf)
        low = 1 if g == 0 else 0
        lax.fori_loop(low, no, lambda k, c: (arrive2(f, wrap(me + k, no)), c)[1], 0, unroll=no <= 16)
        flipped[f] = jnp.concatenate([unpack(f, o) for o in range(no)], axis=0).T

    width = 1024
    copies = []
    for o in range(od):
        pieces = []
        for f in range(nf):
            for c in range(2):
                at = o * half + c * maps
                pieces.append(flipped[f, at : at + keep, :])
        z = jnp.concatenate(pieces, axis=0).astype(BF16)
        for at in range(0, degrees, width):
            cut = slice(at, at + width)
            terms = jnp.dot(z, leg[o, :, cut], preferred_element_type=F32)
            sums = terms[0 : 2 * keep] * shaping_ref[o, 0:1, cut]
            for f in range(1, nf):
                sums = sums + terms[f * 2 * keep : (f + 1) * 2 * keep] * shaping_ref[o, f : f + 1, cut]
            for t in range(width // LANES):
                for c in range(2):
                    row = (at // LANES + t) * 2 + c
                    stage[o, pl.ds(row, keep, stride=tiles2), :] = sums[
                        c * keep : (c + 1) * keep, t * LANES : (t + 1) * LANES
                    ]

        for b in range(keep):
            copy = pltpu.make_async_copy(
                stage.at[o, pl.ds(b * tiles2, tiles2)], out.at[b, o], out_sem.at[o, b]
            )
            copy.start()
            copies.append(copy)

    peers_order(lambda to: copy1(to).wait_send())
    peers_all(lambda f, o: copy2(f, o).wait_send())
    for copy in copies:
        copy.wait()


def hand_over_kernel(source, out, held, sem_in, sem_out):
    keep = source.shape[0]
    fetch = [pltpu.make_async_copy(source.at[b], held.at[b], sem_in.at[b]) for b in range(keep)]
    store = [pltpu.make_async_copy(held.at[b], out.at[b], sem_out.at[b]) for b in range(keep)]
    for copy in fetch:
        copy.start()
    for b in range(keep):
        fetch[b].wait()
        store[b].start()
    for copy in store:
        copy.wait()


def on_device(nf, no, harmonics, legendre, beam_window, order_ids, noise_weight):
    maps, od, _, degrees = harmonics.shape
    _, lats, nlon = noise_weight.shape
    all_lats = legendre.shape[2]
    rows, half, total = no * od * 2, maps * 2, nf * no
    keep = maps // nf
    tiles = degrees // LANES
    leg = jnp.swapaxes(legendre, 1, 2)
    harm = harmonics.reshape(maps, od, 2, tiles, LANES)
    harm = jnp.swapaxes(harm, 2, 3).reshape(maps, od, tiles * 2, LANES)
    hbm = pl.BlockSpec(memory_space=pltpu.HBM)
    span = no * LANES
    ahead = rows * lats * span * 4 <= 8 * 2**20
    dma = pltpu.SemaphoreType.DMA
    out = pl.pallas_call(
        functools.partial(gather_kernel, nf, no),
        out_shape=jax.ShapeDtypeStruct((keep, od, tiles * 2, LANES), F32),
        in_specs=[hbm, hbm, hbm, hbm, hbm],
        out_specs=hbm,
        scratch_shapes=[
            pltpu.SMEM(order_ids.shape, jnp.int32),
            pltpu.VMEM(beam_window.shape, F32),
            pltpu.VMEM(harm.shape, BF16),
            pltpu.VMEM(leg.shape, BF16),
            pltpu.VMEM(noise_weight.shape, F32),
            pltpu.VMEM((rows, nlon), F32),
            pltpu.VMEM((rows, nlon), BF16),
            pltpu.VMEM((rows * lats, rows), F32),
            pltpu.VMEM((rows * 2, span), BF16),
            pltpu.VMEM((rows * lats if ahead else 2 * od * lats, span), F32),
            pltpu.VMEM((no, lats, od * half), F32),
            pltpu.VMEM((no, lats, od * half), F32),
            pltpu.VMEM((nf, no, lats // nf, od * half), F32),
            pltpu.VMEM((nf, no, lats // nf, od * half), F32),
            pltpu.VMEM((nf, od * half, all_lats), F32),
            pltpu.VMEM((od, nf, degrees), F32),
            pltpu.VMEM((od, keep * tiles * 2, LANES), F32),
            dma((5,)),
            dma((no,)),
            dma((no,)),
            dma((total,)),
            dma((total,)),
            dma((od, keep)),
        ],
        compiler_params=pltpu.CompilerParams(
            collective_id=0, has_side_effects=True, vmem_limit_bytes=60 * 2**20
        ),
        name="operator",
    )(order_ids, beam_window, harm, leg, noise_weight)
    out = pl.pallas_call(
        hand_over_kernel,
        out_shape=jax.ShapeDtypeStruct(out.shape, out.dtype),
        in_specs=[hbm],
        out_specs=hbm,
        scratch_shapes=[pltpu.VMEM(out.shape, F32), dma((keep,)), dma((keep,))],
        compiler_params=pltpu.CompilerParams(vmem_limit_bytes=60 * 2**20),
        name="hand_over",
    )(out)
    out = jnp.swapaxes(out.reshape(keep, od, tiles, 2, LANES), 2, 3)
    return out.reshape(keep, od, 2, degrees)


def solution(mesh):
    sizes = dict(mesh.shape)
    return jax.shard_map(
        functools.partial(on_device, sizes["freq"], sizes["order"]),
        mesh=mesh,
        in_specs=(
            P(None, "order", None, None),
            P("order", None, None),
            P(),
            P(),
            P("freq", "order", None),
        ),
        out_specs=P("freq", "order", None, None),
        check_vma=False,
    )
```
